512 devices in a mesh: wide: 64 (over y, z), narrow: 8 (over x, core).
Axes of the slice: x: 4, y: 8, z: 8, core: 2. Of those that a mesh axis runs over, the one named last changes fastest.
Arguments:
- state: float32 [100, 524288], P(None, ('wide', 'narrow')), may hold values from -6 to 6
- neighbours: int32 [4, 524288], P(None, ('wide', 'narrow')), may hold values from 0 to 4863, as said below
- elem_tent: int32 [524288], P(('wide', 'narrow')), may hold values from 0 to 63, as said below
- boundary: int32 [393216], P(('wide', 'narrow')), may hold values from 0 to 1023, as said below
- active: int32 [4, 32768], P(None, ('wide', 'narrow')), may hold values from 0 to 1, as said below
- tent_height: float32 [32768], P(('wide', 'narrow')), may hold values from 0.25 to 1
- volume_op: bfloat16 [100, 100], replicated, may hold values from -0.3125 to 0.3125
- lift_op: bfloat16 [4, 100, 50], replicated, may hold values from -0.875 to 0.875
- trace_op: bfloat16 [4, 50, 100], replicated, may hold values from -0.625 to 0.625
Outputs:
- advanced: float32 [100, 524288], P(None, ('wide', 'narrow'))
The draws below stay inside these ranges and needn't reach their ends.
Inputs may be any that keep to these rules, and one draw needn't show every extreme that they name: `elem_tent`: each tent of a partition holds exactly 16 of its elements. `boundary`: the 768 entries of a partition are distinct local elements; the local face 3 of its k-th entry has neighbours value 4 * 1024 + k. `neighbours`: values below 4096 are g * 1024 + e for a local element e and face g; values 4 * 1024 + k name column k of remote. `active`: at most 24 tents of one partition are pitched in one layer, and in every layer some partition pitches exactly 24.
All inputs are finite; a program needn't handle non-finite values.
Results may differ from the reference program's by a relative error of at most 0.0037.
Values may be sent and summed in bfloat16 or wider, within the bound.
No kernel may reach another device: no remote copies, remote signals or barrier semaphores. Data moves between devices by JAX's collectives and lax.ppermute only.
A program may use at most 64 MiB of HBM per device.

```python
import math
import jax
import jax.numpy as jnp
from jax import lax

COMPS = 100
TRACE = 50
TENT_SIZE = 16
TAYLOR = 4
LAYERS = 4
TENTS_DEV = 64
E_DEV = 1024
BW = 256
BN = 128
HALO = 768
ELEMS = 524288
TENTS = 32768
N_WIDE = 64
N_NARROW = 8
DEVICES = 512


def boundary_perm(key):
    keys = jax.random.split(jax.random.fold_in(key, 99), DEVICES)
    return jax.vmap(lambda sub_key: jax.random.permutation(sub_key, E_DEV))(keys).astype(jnp.int32)


def draw_boundary(key, part):
    perm = boundary_perm(key)
    return perm[:, :HALO].reshape(-1).astype(jnp.int32)


def draw_neighbours(key, part):
    perm = boundary_perm(key)
    key = jax.random.fold_in(key, 5)
    key_faces, key_cells = jax.random.split(key)
    faces = jax.random.randint(key_faces, (4, DEVICES, E_DEV), 0, 4)
    cells = jax.random.randint(key_cells, (4, DEVICES, E_DEV), 0, E_DEV)
    local = (faces * E_DEV + cells).astype(jnp.int32)
    slots = (4 * E_DEV + jnp.arange(HALO)).astype(jnp.int32)
    rows = jnp.arange(DEVICES)[:, None]
    face_three = local[3].at[rows, perm[:, :HALO]].set(jnp.broadcast_to(slots[None, :], (DEVICES, HALO)))
    local = local.at[3].set(face_three)
    return local.reshape(4, DEVICES * E_DEV).astype(jnp.int32)


def draw_elem_tent(key, part):
    key = jax.random.fold_in(key, 7)
    keys = jax.random.split(key, DEVICES)
    perms = jax.vmap(lambda sub_key: jax.random.permutation(sub_key, E_DEV))(keys)
    return (perms // TENT_SIZE).reshape(-1).astype(jnp.int32)


def draw_active(key, part):
    key = jax.random.fold_in(key, 11)
    key_counts, key_top, key_perm = jax.random.split(key, 3)
    mean_count = TENTS_DEV // 8
    counts = jax.random.randint(key_counts, (LAYERS, DEVICES), 1, 2 * mean_count)
    top = jax.random.randint(key_top, (LAYERS,), 0, DEVICES)
    counts = jnp.where(jnp.arange(DEVICES)[None, :] == top[:, None], 3 * mean_count, counts)
    keys = jax.random.split(key_perm, LAYERS * DEVICES)
    perms = jax.vmap(lambda sub_key: jax.random.permutation(sub_key, TENTS_DEV))(keys)
    perms = perms.reshape(LAYERS, DEVICES, TENTS_DEV)
    chosen = (perms < counts[:, :, None]).astype(jnp.int32)
    return chosen.reshape(LAYERS, DEVICES * TENTS_DEV)


def block_levels(own_key, shape, shards, low, top_value):
    gain, own = 1.0, jax.random.fold_in(own_key, 6)
    for axis_at, parts in shards:
        steps = jnp.exp(jax.random.uniform(jax.random.fold_in(own, axis_at), (parts,), jnp.float32, low / len(shards), top_value / len(shards)))
        gain = gain * jnp.repeat(steps, shape[axis_at] // parts).reshape([-1 if axis == axis_at else 1 for axis in range(len(shape))])
    return gain


def bell_draw(stream_key, extent, spread, most, pieces=(), held_as=jnp.bfloat16):
    entries = jax.random.normal(stream_key, extent, jnp.float32) * spread
    if len(pieces) > 0:
        entries = block_levels(stream_key, extent, pieces, -0.22, 0.18) * entries
    return jnp.clip(entries, min=-most, max=most).astype(held_as)


def setup_inputs(seed: int = 0) -> dict:
    splits = jax.random.split(jax.random.key(seed), 10)
    state = bell_draw(splits[0], (COMPS, ELEMS), 1.0, 6.0, ((1, 512),), jnp.float32)
    neighbours = draw_neighbours(jax.random.fold_in(splits[9], 71), 0)
    elem_tent = draw_elem_tent(jax.random.fold_in(splits[9], 71), 0)
    boundary = draw_boundary(jax.random.fold_in(splits[9], 71), 0)
    active = draw_active(jax.random.fold_in(splits[9], 71), 0)
    tent_height = jnp.clip(jnp.exp(math.log(1.0) - 1.3862944 * jax.random.uniform(splits[5], (TENTS,), jnp.float32) ** block_levels(splits[5], (TENTS,), ((0, 512),), -0.2, 0.2)), 0.25, 1.0)
    volume_op = bell_draw(splits[6], (COMPS, COMPS), (4 * COMPS) ** -0.5, 0.3125)
    lift_op = bell_draw(splits[7], (4, COMPS, TRACE), TRACE ** -0.5, 0.875)
    trace_op = bell_draw(splits[8], (4, TRACE, COMPS), COMPS ** -0.5, 0.625)
    return dict(state=state, neighbours=neighbours, elem_tent=elem_tent, boundary=boundary, active=active, tent_height=tent_height, volume_op=volume_op, lift_op=lift_op, trace_op=trace_op)


def face_traces(rounded, trace_op):
    return [jnp.dot(trace_op[face_index], rounded, preferred_element_type=jnp.float32).astype(jnp.bfloat16) for face_index in range(4)]


def advance(values, rounded, neighbour_cols, trace_table, heights, live_mask, volume_op, lift_op):
    source = jnp.zeros(values.shape, jnp.float32)
    for face_index in range(4):
        picked = jnp.take(trace_table, neighbour_cols[face_index], axis=1)
        source = source + jnp.dot(lift_op[face_index], picked, preferred_element_type=jnp.float32)
    summed = values
    current_term = rounded
    for order_index in range(1, TAYLOR + 1):
        product = jnp.dot(volume_op, current_term, preferred_element_type=jnp.float32)
        if order_index == 1:
            product = product + source
        taylor_term = (heights / order_index) * product
        summed = summed + taylor_term
        current_term = taylor_term.astype(jnp.bfloat16)
    return jnp.where(live_mask > 0, summed, values)


def reference(state, neighbours, elem_tent, boundary, active, tent_height, volume_op, lift_op, trace_op):
    device_count = N_WIDE * N_NARROW
    states = state.reshape(COMPS, device_count, E_DEV).transpose(1, 0, 2)
    neighbour_all = neighbours.reshape(4, device_count, E_DEV).transpose(1, 0, 2)
    tent_ids = elem_tent.reshape(device_count, E_DEV)
    boundary_all = boundary.reshape(device_count, HALO)
    active_all = active.reshape(LAYERS, device_count, TENTS_DEV).transpose(1, 0, 2)
    heights_all = tent_height.reshape(device_count, TENTS_DEV)
    for layer_index in range(LAYERS):
        def outgoing_of(pack):
            values, chosen = pack
            edge = jnp.take(values, chosen, axis=1).astype(jnp.bfloat16)
            return jnp.dot(trace_op[3], edge, preferred_element_type=jnp.float32).astype(jnp.bfloat16)

        outgoing = lax.map(outgoing_of, (states, boundary_all))
        grid = outgoing.reshape(N_WIDE, N_NARROW, TRACE, HALO)
        zero_wide = jnp.zeros((1, N_NARROW, TRACE, BW), jnp.bfloat16)
        zero_narrow = jnp.zeros((N_WIDE, 1, TRACE, BN), jnp.bfloat16)
        from_low_wide = jnp.concatenate([zero_wide, grid[:-1, :, :, BW:2 * BW]], axis=0)
        from_high_wide = jnp.concatenate([grid[1:, :, :, :BW], zero_wide], axis=0)
        from_low_narrow = jnp.concatenate([zero_narrow, grid[:, :-1, :, 2 * BW + BN:]], axis=1)
        from_high_narrow = jnp.concatenate([grid[:, 1:, :, 2 * BW:2 * BW + BN], zero_narrow], axis=1)
        received = jnp.concatenate([from_low_wide, from_high_wide, from_low_narrow, from_high_narrow], axis=3)
        received = received.reshape(device_count, TRACE, HALO)

        def one_device(pack):
            values, neighbour_cols, tents_here, active_here, heights_here, remote = pack
            rounded = values.astype(jnp.bfloat16)
            trace_table = jnp.concatenate(face_traces(rounded, trace_op) + [remote], axis=1)
            heights = heights_here[tents_here]
            live_mask = active_here[layer_index][tents_here]
            return advance(values, rounded, neighbour_cols, trace_table, heights, live_mask, volume_op, lift_op)

        states = lax.map(one_device, (states, neighbour_all, tent_ids, active_all, heights_all, received))
    return states.transpose(1, 0, 2).reshape(COMPS, device_count * E_DEV)
```

```python
import functools

import jax
import jax.numpy as jnp
from jax import lax
from jax.experimental import pallas as pl
from jax.experimental.pallas import tpu as pltpu
from jax.sharding import PartitionSpec as P

TAYLOR = 4
TENT_SIZE = 16
MAX_TENTS = 24
MAX_LIVE = TENT_SIZE * MAX_TENTS
ROWS = 64
BLOCK = 256
CHUNK = 512
LANES = 128
VMEM = 24 * 2**20
PHASES = (("wide", 1), ("narrow", 1), ("wide", 0), ("narrow", 0))
BF16, F32, I32 = jnp.bfloat16, jnp.float32, jnp.int32


def mm(left, right):
    return jnp.dot(left, right, preferred_element_type=F32)


def mm_t(left, right):
    return lax.dot_general(left, right, (((1,), (1,)), ((), ())), preferred_element_type=F32)


def low_of(index):
    return index & (BLOCK - 1)


def high_of(index):
    return index >> 8


def hot(index, depth):
    low, high = low_of(index), high_of(index)
    rows = lax.broadcasted_iota(I32, (BLOCK, index.shape[1]), 0).astype(F32).astype(BF16)
    parts = []
    for b in range(-(-depth // BLOCK)):
        here = jnp.where(high == b, low, -1).astype(F32).astype(BF16)
        count = min(BLOCK, depth - b * BLOCK)
        parts.append(jnp.where(rows[:count] == here, jnp.ones((), BF16), jnp.zeros((), BF16)))
    return parts[0] if len(parts) == 1 else jnp.concatenate(parts, axis=0)


def choose(found, key, first, rows, default=None):
    count = found.shape[0] // rows
    total = found[(count - 1) * rows :]
    if default is not None:
        total = jnp.where(key == first + count - 1, total, default)
    for b in range(count - 2, -1, -1):
        total = jnp.where(key == first + b, found[b * rows : (b + 1) * rows], total)
    return total


def stack(table):
    return jnp.concatenate([table[:, at : at + BLOCK] for at in range(0, table.shape[1], BLOCK)], axis=0)


def pick(table, low, high, first=0, default=0.0):
    return choose(mm(stack(table), hot(low, BLOCK)), high, first, table.shape[0], default)


def two_parts(values):
    rows = values.shape[0]
    start = -(-rows // 16) * 16
    top = values.astype(BF16).astype(F32)
    gap = jnp.zeros((start - rows, values.shape[1]), F32)
    return jnp.concatenate([jnp.concatenate([top, gap], axis=0), values - top], axis=0).astype(BF16), start


def three_parts(values):
    top = values.astype(BF16).astype(F32)
    mid = (values - top).astype(BF16).astype(F32)
    return top, mid, values - top - mid


def even(axis):
    return lax.axis_index(axis) % 2 == 0


def by_phase(columns):
    half, quarter = columns.shape[1] // 3, columns.shape[1] // 6
    low, high = columns[:, :half], columns[:, half : 2 * half]
    left, right = columns[:, 2 * half : 2 * half + quarter], columns[:, 2 * half + quarter :]
    wide, narrow = even("wide"), even("narrow")
    return jnp.concatenate(
        [
            jnp.where(wide, low, high),
            jnp.where(wide, high, low),
            jnp.where(narrow, left, right),
            jnp.where(narrow, right, left),
        ],
        axis=1,
    )


def remote_by_phase(near, local_columns, halo):
    half, quarter = halo // 3, halo // 6
    at = near - local_columns
    wide, narrow = even("wide"), even("narrow")
    in_wide = jnp.where(wide, at, jnp.where(at < half, at + half, at - half))
    in_narrow = jnp.where(narrow, at, jnp.where(at < 2 * half + quarter, at + quarter, at - quarter))
    return jnp.where(at < 0, near, local_columns + jnp.where(at < 2 * half, in_wide, in_narrow))


def store_blocks(out, refs):
    at = 0
    for ref in refs:
        width = ref.shape[1]
        ref[...] = out[:, at : at + width].astype(BF16)
        at += width


def row_of(ref):
    return jnp.concatenate([ref[i : i + 1, :] for i in range(ref.shape[0])], axis=1)


def face_rows(op, face):
    gap = jnp.zeros((ROWS - op.shape[0], op.shape[2]), F32)
    return jnp.concatenate([op[:, face, :].astype(F32), gap], axis=0)


def first_kernel(*refs):
    count = (len(refs) - 4) // 2
    inputs, blocks, held, sems = refs[:count], refs[count : count + 4], refs[count + 4 : -1], refs[-1]
    copies = [pltpu.make_async_copy(src, dst, sems.at[i]) for i, (src, dst) in enumerate(zip(inputs, held))]
    for copy in copies:
        copy.start()
    for copy in copies:
        copy.wait()
    state, boundary, trace_op = held[:3]
    traces = mm(face_rows(trace_op, 3).astype(BF16), state[...].astype(BF16)).astype(BF16)
    at = by_phase(row_of(boundary))
    store_blocks(pick(traces, low_of(at), high_of(at)), blocks)


def make_index(neighbours, elem_tent, boundary, active, height, compact, ranks, sent):
    tent = row_of(elem_tent)
    elems = tent.shape[1]
    tents = height.shape[1]
    layers = active.shape[0]
    act = active[...].astype(F32)
    top, mid, low = three_parts(height[...])
    row = lax.broadcasted_iota(I32, (2 * layers, tents), 0)
    high_rows = jnp.where(row == 0, top, jnp.where(row == 1, mid, jnp.where(row == 2, low, 0.0)))
    found = mm(jnp.concatenate([act, act, high_rows], axis=0).astype(BF16), hot(tent, tents))
    live, high_rows = found[: 2 * layers], found[2 * layers :]
    upto = jnp.where(
        lax.broadcasted_iota(I32, (LANES, LANES), 0) <= lax.broadcasted_iota(I32, (LANES, LANES), 1), 1.0, 0.0
    ).astype(BF16)
    chunks = [live[:, at : at + LANES] for at in range(0, elems, LANES)]
    counts = mm(jnp.concatenate(chunks, axis=0).astype(BF16), upto)
    offset = jnp.zeros((2 * layers, 1), F32)
    parts = []
    for c in range(len(chunks)):
        part = counts[c * 2 * layers : (c + 1) * 2 * layers]
        parts.append(part + offset)
        offset = offset + part[:, LANES - 1 :]
    place = jnp.where(live > 0.5, jnp.concatenate(parts, axis=1), 0.0).astype(I32)
    ranks[...] = place - 1
    row = lax.broadcasted_iota(I32, (2 * layers, elems), 0)
    digits = jnp.where(row < layers, low_of(place), high_of(place)).astype(F32)
    table = jnp.concatenate([digits, jnp.zeros_like(digits)], axis=0).astype(BF16)
    at = by_phase(row_of(boundary))
    found = pick(table, low_of(at), high_of(at))
    sent[...] = (found[:layers] + BLOCK * found[layers : 2 * layers]).astype(I32) - 1

    near = remote_by_phase(neighbours[...], 4 * elems, at.shape[1])
    near = jnp.concatenate([near, near], axis=0)
    near = jnp.where(row < layers, low_of(near), high_of(near)).astype(F32)
    elem = lax.broadcasted_iota(I32, (2 * layers, elems), 1)
    own = jnp.where(row == 3, low_of(elem).astype(F32), jnp.where(row == 4, high_of(elem).astype(F32), 0.0))
    rows16 = jnp.concatenate([near, high_rows + own], axis=0)
    count = MAX_LIVE // LANES
    for l in range(0, layers, 2):
        tables, columns = [], []
        for m in (l, l + 1):
            rank = place[m : m + 1] - 1
            tables += [jnp.where(rank >> 7 == b, rows16, 0.0) for b in range(count)]
            columns.append(hot(jnp.where(rank < 0, -1, rank & (LANES - 1)), LANES))
        found = mm_t(jnp.concatenate(tables, axis=0).astype(BF16), jnp.concatenate(columns, axis=0))
        for m in (0, 1):
            for b in range(count):
                at = 16 * (m * count + b)
                compact[l + m, :, b * LANES : (b + 1) * LANES] = found[at : at + 16, m * LANES : (m + 1) * LANES]


def whole(compact, row, count=1):
    rows = [compact[i : i + 1] for i in range(row, row + count)]
    return (rows[0] if count == 1 else jnp.concatenate(rows, axis=1)).astype(I32)


def by_face(columns):
    n = columns.shape[1] // 4
    return jnp.concatenate([columns[:, g * n : (g + 1) * n] for g in range(4)], axis=0)


def local_part(values, compact, volume, lift, trace, base, kept):
    comps, elems = values.shape
    blocks = elems // BLOCK
    parts, rows = two_parts(values)
    top = stack(parts[:rows])
    low = jnp.concatenate([whole(compact, 11), whole(compact, 0, 4)], axis=1)
    high = jnp.concatenate([whole(compact, 12), whole(compact, 4, 4)], axis=1)
    block, face = high & (blocks - 1), high // blocks
    near = []
    for at in range(0, low.shape[1], CHUNK):
        here = slice(at, at + CHUNK)
        near.append(choose(mm(top, hot(low[:, here], BLOCK)), block[:, here], 0, rows)[:comps].astype(BF16))
    near = jnp.concatenate(near, axis=1)
    mine, near, face = near[:, :MAX_LIVE], near[:, MAX_LIVE:], face[:, MAX_LIVE:]
    picked = []
    for at in range(0, near.shape[1], CHUNK):
        here = slice(at, at + CHUNK)
        picked.append(choose(mm(trace[...], near[:, here]), face[:, here], 0, ROWS, 0.0))
    picked = by_face(jnp.concatenate(picked, axis=1)).astype(BF16)
    if kept is not None:
        rest = stack(jnp.concatenate([parts[rows:].astype(F32), jnp.zeros((rows - comps, elems), F32)], axis=0))
        own = slice(0, MAX_LIVE)
        rest = choose(mm(rest.astype(BF16), hot(low[:, own], BLOCK)), block[:, own], 0, rows)
        kept[...] = mine.astype(F32) + rest[:comps]
    base[...] = mm(volume[...], mine) + mm(lift[...], picked)


def local_first_kernel(
    state, neighbours, elem_tent, boundary, active, height, volume, lift_op, trace_op,
    compact, ranks, sent, base, kept, lift, trace,
):
    make_index(neighbours, elem_tent, boundary, active, height, compact, ranks, sent)
    lifts = jnp.concatenate([face_rows(lift_op, g) for g in range(4)], axis=0).astype(BF16)
    comps = lifts.shape[1]
    diagonal = lax.broadcasted_iota(I32, (comps, comps), 0) == lax.broadcasted_iota(I32, (comps, comps), 1)
    lift[...] = mm_t(jnp.where(diagonal, 1.0, 0.0).astype(BF16), lifts).astype(BF16)
    trace[...] = jnp.concatenate([face_rows(trace_op, g) for g in range(4)], axis=0).astype(BF16)
    local_part(state[...], compact[0], volume, lift, trace, base, kept)


def scatter(delta, rank):
    parts, second = two_parts(delta)
    found = mm(parts, hot(rank, MAX_LIVE))
    return found[: delta.shape[0]] + found[second:]


def local_kernel(layer, state, delta, compact, ranks, volume, lift, trace, new_state, base, kept=None):
    values = state[...] + scatter(delta[...], ranks[layer - 1 : layer])
    new_state[...] = values
    local_part(values, compact[layer], volume, lift, trace, base, kept)


def taylor_terms(received, compact, base, volume, lift):
    remote = jnp.concatenate([ref[...] for ref in received], axis=1)
    first_block = 4 * 1024 // BLOCK
    picked = by_face(pick(remote, whole(compact, 0, 4), whole(compact, 4, 4), first_block)).astype(BF16)
    heights = compact[8:9] + compact[9:10] + compact[10:11]
    term = heights * (base[...] + mm(lift[...], picked))
    total = term
    for order in range(2, TAYLOR + 1):
        term = (heights / order) * mm(volume[...], term.astype(BF16))
        total = total + term
    return total


def advance_kernel(layer, r0, r1, r2, r3, o0, o1, o2, o3, compact, base, kept, sent, volume, lift, trace, delta, *outgoing):
    total = taylor_terms((r0, r1, r2, r3), compact[layer], base, volume, lift)
    delta[...] = total
    traces = mm(trace[3 * ROWS :, :], (kept[...] + total).astype(BF16))
    rest = -MAX_LIVE % BLOCK
    table = jnp.concatenate([traces, jnp.zeros((ROWS, rest), F32)], axis=1).astype(BF16)
    place = sent[layer : layer + 1]
    found = pick(table, low_of(place), high_of(place))
    before = jnp.concatenate([o0[...], o1[...], o2[...], o3[...]], axis=1).astype(F32)
    store_blocks(jnp.where(place >= 0, found, before), outgoing)


def last_kernel(layer, r0, r1, r2, r3, compact, base, ranks, volume, lift, state, advanced, held, sems):
    parts, second = two_parts(taylor_terms((r0, r1, r2, r3), compact[layer], base, volume, lift))
    comps, elems = state.shape
    copies = []
    for c in range(elems // BLOCK):
        here = slice(c * BLOCK, (c + 1) * BLOCK)
        found = mm(parts, hot(ranks[layer : layer + 1, here], MAX_LIVE))
        held[:, here] = state[:, here] + found[:comps] + found[second:]
        copies.append(pltpu.make_async_copy(held.at[:, here], advanced.at[:, here], sems.at[c]))
        copies[-1].start()
    for copy in copies:
        copy.wait()


def call(kernel, outs, args, flops):
    outs = [jax.ShapeDtypeStruct(shape, dtype) for shape, dtype in outs]
    return pl.pallas_call(
        kernel,
        out_shape=outs,
        compiler_params=pltpu.CompilerParams(vmem_limit_bytes=VMEM),
        cost_estimate=pl.CostEstimate(flops=flops, bytes_accessed=2**20, transcendentals=0),
    )(*args)


def swapped(block, axis, first):
    pairs = [(i, i + 1) for i in range(first, lax.axis_size(axis) - 1, 2)]
    return lax.ppermute(block, axis, pairs + [(j, i) for i, j in pairs])


def exchange(outgoing):
    wide_1, wide_0, narrow_1, narrow_0 = outgoing
    wide_1, narrow_1, wide_0, narrow_0 = [
        swapped(block, axis, first)
        for block, (axis, first) in zip((wide_1, narrow_1, wide_0, narrow_0), PHASES)
    ]
    return wide_1, wide_0, narrow_1, narrow_0


def local(state, neighbours, elem_tent, boundary, active, tent_height, volume_op, lift_op, trace_op):
    comps, elems = state.shape
    layers = active.shape[0]
    halo = boundary.shape[0]
    wide_len = halo // 3
    narrow_len = wide_len // 2
    boundary = boundary.reshape(-1, LANES)
    elem_tent = elem_tent.reshape(-1, LANES)
    tent_height = tent_height.reshape(1, -1)

    blocks = [((ROWS, width), BF16) for width in (wide_len, wide_len, narrow_len, narrow_len)]
    live = ((comps, MAX_LIVE), F32)
    all_columns = ((comps, elems), F32)
    args = (
        state, boundary, trace_op.transpose(1, 0, 2), neighbours, elem_tent, active, tent_height, volume_op,
        lift_op.transpose(2, 0, 1),
    )
    held = [jax.ShapeDtypeStruct(arg.shape, arg.dtype) for arg in args]
    outs = pl.pallas_call(
        first_kernel,
        in_specs=[pl.BlockSpec(memory_space=pltpu.MemorySpace.HBM)] * len(args),
        out_shape=[jax.ShapeDtypeStruct(shape, dtype) for shape, dtype in blocks] + held,
        scratch_shapes=[pltpu.SemaphoreType.DMA((len(args),))],
        compiler_params=pltpu.CompilerParams(vmem_limit_bytes=VMEM),
    )(*[pltpu.with_memory_space_constraint(arg, pltpu.MemorySpace.HBM) for arg in args])
    outgoing = outs[:4]
    state, boundary, trace, neighbours, elem_tent, active, tent_height, volume_op, lift = outs[4:]
    received = exchange(outgoing)
    compact, ranks, sent, base, kept, lift, trace = call(
        local_first_kernel,
        [
            ((layers, 16, MAX_LIVE), F32),
            ((2 * layers, elems), I32),
            ((layers, halo), I32),
            live,
            live,
            ((comps, 4 * ROWS), BF16),
            ((4 * ROWS, comps), BF16),
        ],
        (state, neighbours, elem_tent, boundary, active, tent_height, volume_op, lift, trace),
        10**9,
    )
    for layer in range(layers - 1):
        delta, *outgoing = call(
            functools.partial(advance_kernel, layer),
            [live] + blocks,
            (*received, *outgoing, compact, base, kept, sent, volume_op, lift, trace),
            10**9,
        )
        received = exchange(outgoing)
        state, base, *rest = call(
            functools.partial(local_kernel, layer + 1),
            [all_columns, live] + [live] * (layer + 2 < layers),
            (state, delta, compact, ranks, volume_op, lift, trace),
            10**9,
        )
        kept = rest[0] if rest else None
    return pl.pallas_call(
        functools.partial(last_kernel, layers - 1),
        out_specs=pl.BlockSpec(memory_space=pltpu.MemorySpace.HBM),
        out_shape=jax.ShapeDtypeStruct((comps, elems), F32),
        scratch_shapes=[pltpu.VMEM((comps, elems), F32), pltpu.SemaphoreType.DMA((elems // BLOCK,))],
        compiler_params=pltpu.CompilerParams(vmem_limit_bytes=VMEM),
    )(*received, compact, base, ranks, volume_op, lift, state)


def solution(mesh):
    both = ("wide", "narrow")
    return jax.shard_map(
        local,
        mesh=mesh,
        in_specs=(P(None, both), P(None, both), P(both), P(both), P(None, both), P(both), P(), P(), P()),
        out_specs=P(None, both),
        check_vma=False,
    )
```

```python
import functools

import jax
import jax.numpy as jnp
from jax import lax
from jax.experimental import pallas as pl
from jax.experimental.pallas import tpu as pltpu
from jax.sharding import PartitionSpec as P

TENT_SIZE = 16
MAX_TENTS = 24
MAX_LIVE = TENT_SIZE * MAX_TENTS
ROWS = 64
BLOCK = 256
SPLIT = 256
CHUNK = 512
LANES = 128
VMEM = 24 * 2**20
POWER_ROWS = 112
PHASES = (("wide", 1), ("narrow", 1), ("wide", 0), ("narrow", 0))
BF16, F32, I32 = jnp.bfloat16, jnp.float32, jnp.int32


def mm(left, right):
    return jnp.dot(left, right, preferred_element_type=F32)


def mm_t(left, right):
    return lax.dot_general(left, right, (((1,), (1,)), ((), ())), preferred_element_type=F32)


def low_of(index):
    return index & (BLOCK - 1)


def high_of(index):
    return index >> 8


def hot(index, depth):
    low, high = low_of(index), high_of(index)
    rows = lax.broadcasted_iota(I32, (BLOCK, index.shape[1]), 0).astype(F32).astype(BF16)
    parts = []
    for b in range(-(-depth // BLOCK)):
        here = jnp.where(high == b, low, -1).astype(F32).astype(BF16)
        count = min(BLOCK, depth - b * BLOCK)
        parts.append(jnp.where(rows[:count] == here, jnp.ones((), BF16), jnp.zeros((), BF16)))
    return parts[0] if len(parts) == 1 else jnp.concatenate(parts, axis=0)


def choose(found, key, first, rows, default=None):
    count = found.shape[0] // rows
    total = found[(count - 1) * rows :]
    if default is not None:
        total = jnp.where(key == first + count - 1, total, default)
    for b in range(count - 2, -1, -1):
        total = jnp.where(key == first + b, found[b * rows : (b + 1) * rows], total)
    return total


def stack(table):
    return jnp.concatenate([table[:, at : at + BLOCK] for at in range(0, table.shape[1], BLOCK)], axis=0)


def pick(table, low, high, first=0, default=0.0):
    return choose(mm(stack(table), hot(low, BLOCK)), high, first, table.shape[0], default)


def two_parts(values):
    rows = values.shape[0]
    start = -(-rows // 16) * 16
    top = values.astype(BF16).astype(F32)
    gap = jnp.zeros((start - rows, values.shape[1]), F32)
    return jnp.concatenate([jnp.concatenate([top, gap], axis=0), values - top], axis=0).astype(BF16), start


def three_parts(values):
    top = values.astype(BF16).astype(F32)
    mid = (values - top).astype(BF16).astype(F32)
    return top, mid, values - top - mid


def even(axis):
    return lax.axis_index(axis) % 2 == 0


def by_phase(columns):
    half, quarter = columns.shape[1] // 3, columns.shape[1] // 6
    low, high = columns[:, :half], columns[:, half : 2 * half]
    left, right = columns[:, 2 * half : 2 * half + quarter], columns[:, 2 * half + quarter :]
    wide, narrow = even("wide"), even("narrow")
    return jnp.concatenate(
        [
            jnp.where(wide, low, high),
            jnp.where(wide, high, low),
            jnp.where(narrow, left, right),
            jnp.where(narrow, right, left),
        ],
        axis=1,
    )


def remote_by_phase(near, local_columns, halo):
    half, quarter = halo // 3, halo // 6
    at = near - local_columns
    wide, narrow = even("wide"), even("narrow")
    in_wide = jnp.where(wide, at, jnp.where(at < half, at + half, at - half))
    in_narrow = jnp.where(narrow, at, jnp.where(at < 2 * half + quarter, at + quarter, at - quarter))
    return jnp.where(at < 0, near, local_columns + jnp.where(at < 2 * half, in_wide, in_narrow))


def store_blocks(out, refs):
    at = 0
    for ref in refs:
        width = ref.shape[1]
        ref[...] = out[:, at : at + width].astype(BF16)
        at += width


def row_of(ref):
    return jnp.concatenate([ref[i : i + 1, :] for i in range(ref.shape[0])], axis=1)


def face_rows(op, face):
    gap = jnp.zeros((ROWS - op.shape[0], op.shape[2]), F32)
    return jnp.concatenate([op[:, face, :].astype(F32), gap], axis=0)


def first_kernel(*refs):
    count = (len(refs) - 4) // 2
    inputs, blocks, held, sems = refs[:count], refs[count : count + 4], refs[count + 4 : -1], refs[-1]
    copies = [pltpu.make_async_copy(src, dst, sems.at[i]) for i, (src, dst) in enumerate(zip(inputs, held))]
    for copy in copies:
        copy.start()
    state, boundary, trace_op = held[:3]
    copies[1].wait()
    at = by_phase(row_of(boundary))
    chosen, high = hot(low_of(at), BLOCK), high_of(at)
    copies[2].wait()
    face = face_rows(trace_op, 3).astype(BF16)
    copies[0].wait()
    traces = mm(face, state[...].astype(BF16)).astype(BF16)
    store_blocks(choose(mm(stack(traces), chosen), high, 0, ROWS), blocks)
    for copy in copies[3:]:
        copy.wait()


def make_index(neighbours, elem_tent, boundary, active, height, compact, ranks, sent):
    tent = row_of(elem_tent)
    elems = tent.shape[1]
    tents = height.shape[1]
    layers = active.shape[0]
    act = active[...].astype(F32)
    top, mid, low = three_parts(height[...])
    row = lax.broadcasted_iota(I32, (2 * layers, tents), 0)
    high_rows = jnp.where(row == 0, top, jnp.where(row == 1, mid, jnp.where(row == 2, low, 0.0)))
    found = mm(jnp.concatenate([act, act, high_rows], axis=0).astype(BF16), hot(tent, tents))
    live, high_rows = found[: 2 * layers], found[2 * layers :]
    upto = jnp.where(
        lax.broadcasted_iota(I32, (LANES, LANES), 0) <= lax.broadcasted_iota(I32, (LANES, LANES), 1), 1.0, 0.0
    ).astype(BF16)
    chunks = [live[:, at : at + LANES] for at in range(0, elems, LANES)]
    counts = mm(jnp.concatenate(chunks, axis=0).astype(BF16), upto)
    offset = jnp.zeros((2 * layers, 1), F32)
    parts = []
    for c in range(len(chunks)):
        part = counts[c * 2 * layers : (c + 1) * 2 * layers]
        parts.append(part + offset)
        offset = offset + part[:, LANES - 1 :]
    place = jnp.where(live > 0.5, jnp.concatenate(parts, axis=1), 0.0).astype(I32)
    ranks[...] = place - 1
    row = lax.broadcasted_iota(I32, (2 * layers, elems), 0)
    digits = jnp.where(row < layers, low_of(place), high_of(place)).astype(F32)
    table = jnp.concatenate([digits, jnp.zeros_like(digits)], axis=0).astype(BF16)
    at = by_phase(row_of(boundary))
    found = pick(table, low_of(at), high_of(at))
    sent[...] = (found[:layers] + BLOCK * found[layers : 2 * layers]).astype(I32) - 1

    near = remote_by_phase(neighbours[...], 4 * elems, at.shape[1])
    near = jnp.concatenate([near, near], axis=0)
    near = jnp.where(row < layers, low_of(near), high_of(near)).astype(F32)
    elem = lax.broadcasted_iota(I32, (2 * layers, elems), 1)
    own = jnp.where(row == 3, low_of(elem).astype(F32), jnp.where(row == 4, high_of(elem).astype(F32), 0.0))
    rows16 = jnp.concatenate([near, high_rows + own], axis=0)
    count = MAX_LIVE // LANES
    for l in range(0, layers, 2):
        tables, columns = [], []
        for m in (l, l + 1):
            rank = place[m : m + 1] - 1
            tables += [jnp.where(rank >> 7 == b, rows16, 0.0) for b in range(count)]
            columns.append(hot(jnp.where(rank < 0, -1, rank & (LANES - 1)), LANES))
        found = mm_t(jnp.concatenate(tables, axis=0).astype(BF16), jnp.concatenate(columns, axis=0))
        for m in (0, 1):
            for b in range(count):
                at = 16 * (m * count + b)
                compact[l + m, :, b * LANES : (b + 1) * LANES] = found[at : at + 16, m * LANES : (m + 1) * LANES]
            compact[l + m, 13:14, :LANES] = jnp.broadcast_to(offset[l + m : l + m + 1], (1, LANES))


def whole(compact, row, count, here):
    rows = [compact[i : i + 1, here] for i in range(row, row + count)]
    return (rows[0] if count == 1 else jnp.concatenate(rows, axis=1)).astype(I32)


def many(compact):
    return jnp.max(compact[13:14, :LANES]) > SPLIT


FIRST, OTHERS = slice(0, SPLIT), slice(SPLIT, MAX_LIVE)


def by_face(columns):
    n = columns.shape[1] // 4
    return jnp.concatenate([columns[:, g * n : (g + 1) * n] for g in range(4)], axis=0)


def local_part(values, compact, here, volume, lift, trace, base, kept):
    comps, elems = values.shape
    blocks = elems // BLOCK
    count = here.stop - here.start
    parts, rows = two_parts(values)
    top = stack(parts[:rows])
    low = jnp.concatenate([whole(compact, 11, 1, here), whole(compact, 0, 4, here)], axis=1)
    high = jnp.concatenate([whole(compact, 12, 1, here), whole(compact, 4, 4, here)], axis=1)
    block, face = high & (blocks - 1), high // blocks
    near = []
    for at in range(0, low.shape[1], CHUNK):
        now = slice(at, at + CHUNK)
        near.append(choose(mm(top, hot(low[:, now], BLOCK)), block[:, now], 0, rows)[:comps].astype(BF16))
    near = jnp.concatenate(near, axis=1)
    mine, near, face = near[:, :count], near[:, count:], face[:, count:]
    picked = []
    for at in range(0, near.shape[1], CHUNK):
        now = slice(at, at + CHUNK)
        picked.append(choose(mm(trace[...], near[:, now]), face[:, now], 0, ROWS, 0.0))
    picked = by_face(jnp.concatenate(picked, axis=1)).astype(BF16)
    if kept is not None:
        rest = stack(jnp.concatenate([parts[rows:].astype(F32), jnp.zeros((rows - comps, elems), F32)], axis=0))
        rest = choose(mm(rest.astype(BF16), hot(low[:, :count], BLOCK)), block[:, :count], 0, rows)
        kept[:, here] = mine.astype(F32) + rest[:comps]
    base[:, here] = mm(volume[...], mine) + mm(lift[...], picked)


def local_parts(values, compact, *refs):
    local_part(values[...], compact, FIRST, *refs)

    @pl.when(many(compact))
    def _():
        local_part(values[...], compact, OTHERS, *refs)


def local_first_kernel(
    state, neighbours, elem_tent, boundary, active, height, volume, lift_op, trace_op,
    compact, ranks, sent, base, kept, lift, trace, powers,
):
    powers[...] = powers_of(volume[...])
    make_index(neighbours, elem_tent, boundary, active, height, compact, ranks, sent)
    lifts = jnp.concatenate([face_rows(lift_op, g) for g in range(4)], axis=0).astype(BF16)
    comps = lifts.shape[1]
    diagonal = lax.broadcasted_iota(I32, (comps, comps), 0) == lax.broadcasted_iota(I32, (comps, comps), 1)
    lift[...] = mm_t(jnp.where(diagonal, 1.0, 0.0).astype(BF16), lifts).astype(BF16)
    trace[...] = jnp.concatenate([face_rows(trace_op, g) for g in range(4)], axis=0).astype(BF16)
    local_parts(state, compact[0], volume, lift, trace, base, kept)


def scatter(delta, rank, here):
    parts, second = two_parts(delta)
    found = mm(parts, hot(rank - here.start, delta.shape[1]))
    return found[: delta.shape[0]] + found[second:]


def local_kernel(layer, state, delta, compact, ranks, volume, lift, trace, new_state, base, kept=None):
    rank = ranks[layer - 1 : layer]
    new_state[...] = state[...] + scatter(delta[:, FIRST], rank, FIRST)

    @pl.when(many(compact[layer - 1]))
    def _():
        new_state[...] = new_state[...] + scatter(delta[:, OTHERS], rank, OTHERS)

    local_parts(new_state, compact[layer], volume, lift, trace, base, kept)


def powers_of(volume):
    gap = jnp.zeros((POWER_ROWS - volume.shape[0], volume.shape[1]), F32)
    parts = [volume.astype(F32)]
    for _ in range(2):
        power = sum(mm(part.astype(BF16), volume) for part in parts[-2:])
        top = power.astype(BF16).astype(F32)
        parts += [top, power - top]
    return jnp.concatenate([half for part in parts for half in (part, gap)], axis=0).astype(BF16)


def taylor_terms(received, compact, here, base, powers, lift):
    remote = jnp.concatenate([ref[...] for ref in received], axis=1)
    first_block = 4 * 1024 // BLOCK
    picked = by_face(pick(remote, whole(compact, 0, 4, here), whole(compact, 4, 4, here), first_block)).astype(BF16)
    heights = compact[8:9, here] + compact[9:10, here] + compact[10:11, here]
    first = heights * (base[:, here] + mm(lift[...], picked))
    found = mm(powers[...], first.astype(BF16))
    comps = first.shape[0]
    products = [found[at : at + comps] for at in range(0, found.shape[0], POWER_ROWS)]
    total, scale = first, 1.0
    for order, product in ((2, products[0]), (3, products[1] + products[2]), (4, products[3] + products[4])):
        scale = scale * (heights / order)
        total = total + scale * product
    return total


def advance_kernel(layer, r0, r1, r2, r3, o0, o1, o2, o3, compact, base, kept, sent, powers, lift, trace, delta, *outgoing):
    rows = compact[layer]

    def part(here, before):
        place = sent[layer : layer + 1] - here.start
        chosen = hot(place, here.stop - here.start)
        total = taylor_terms((r0, r1, r2, r3), rows, here, base, powers, lift)
        delta[:, here] = total
        traces = mm(trace[3 * ROWS :, :], (kept[:, here] + total).astype(BF16)).astype(BF16)
        before = jnp.concatenate([ref[...] for ref in before], axis=1).astype(F32)
        inside = jnp.logical_and(place >= 0, place < here.stop - here.start)
        store_blocks(jnp.where(inside, mm(traces, chosen), before), outgoing)

    part(FIRST, (o0, o1, o2, o3))

    @pl.when(many(rows))
    def _():
        part(OTHERS, outgoing)


def last_kernel(layer, r0, r1, r2, r3, compact, base, ranks, powers, lift, state, advanced, held, sem):
    rows, rank = compact[layer], ranks[layer : layer + 1]

    def part(here, before):
        total = taylor_terms((r0, r1, r2, r3), rows, here, base, powers, lift)
        held[...] = before[...] + scatter(total, rank, here)

    part(FIRST, state)

    @pl.when(many(rows))
    def _():
        part(OTHERS, held)

    copy = pltpu.make_async_copy(held, advanced, sem)
    copy.start()
    copy.wait()


def call(kernel, outs, args, flops):
    outs = [jax.ShapeDtypeStruct(shape, dtype) for shape, dtype in outs]
    return pl.pallas_call(
        kernel,
        out_shape=outs,
        compiler_params=pltpu.CompilerParams(vmem_limit_bytes=VMEM),
        cost_estimate=pl.CostEstimate(flops=flops, bytes_accessed=2**20, transcendentals=0),
    )(*args)


def swapped(block, axis, first):
    pairs = [(i, i + 1) for i in range(first, lax.axis_size(axis) - 1, 2)]
    return lax.ppermute(block, axis, pairs + [(j, i) for i, j in pairs])


def exchange(outgoing):
    wide_1, wide_0, narrow_1, narrow_0 = outgoing
    wide_1, narrow_1, wide_0, narrow_0 = [
        swapped(block, axis, first)
        for block, (axis, first) in zip((wide_1, narrow_1, wide_0, narrow_0), PHASES)
    ]
    return wide_1, wide_0, narrow_1, narrow_0


def local(state, neighbours, elem_tent, boundary, active, tent_height, volume_op, lift_op, trace_op):
    comps, elems = state.shape
    layers = active.shape[0]
    halo = boundary.shape[0]
    wide_len = halo // 3
    narrow_len = wide_len // 2
    boundary = boundary.reshape(-1, LANES)
    elem_tent = elem_tent.reshape(-1, LANES)
    tent_height = tent_height.reshape(1, -1)

    blocks = [((ROWS, width), BF16) for width in (wide_len, wide_len, narrow_len, narrow_len)]
    live = ((comps, MAX_LIVE), F32)
    all_columns = ((comps, elems), F32)
    args = (
        state, boundary, trace_op.transpose(1, 0, 2), neighbours, elem_tent, active, tent_height, volume_op,
        lift_op.transpose(2, 0, 1),
    )
    held = [jax.ShapeDtypeStruct(arg.shape, arg.dtype) for arg in args]
    outs = pl.pallas_call(
        first_kernel,
        in_specs=[pl.BlockSpec(memory_space=pltpu.MemorySpace.HBM)] * len(args),
        out_shape=[jax.ShapeDtypeStruct(shape, dtype) for shape, dtype in blocks] + held,
        scratch_shapes=[pltpu.SemaphoreType.DMA((len(args),))],
        compiler_params=pltpu.CompilerParams(vmem_limit_bytes=VMEM),
    )(*[pltpu.with_memory_space_constraint(arg, pltpu.MemorySpace.HBM) for arg in args])
    outgoing = outs[:4]
    state, boundary, trace, neighbours, elem_tent, active, tent_height, volume_op, lift = outs[4:]
    received = exchange(outgoing)
    compact, ranks, sent, base, kept, lift, trace, powers = call(
        local_first_kernel,
        [
            ((layers, 16, MAX_LIVE), F32),
            ((2 * layers, elems), I32),
            ((layers, halo), I32),
            live,
            live,
            ((comps, 4 * ROWS), BF16),
            ((4 * ROWS, comps), BF16),
            ((5 * POWER_ROWS, comps), BF16),
        ],
        (state, neighbours, elem_tent, boundary, active, tent_height, volume_op, lift, trace),
        10**9,
    )
    for layer in range(layers - 1):
        delta, *outgoing = call(
            functools.partial(advance_kernel, layer),
            [live] + blocks,
            (*received, *outgoing, compact, base, kept, sent, powers, lift, trace),
            10**9,
        )
        received = exchange(outgoing)
        state, base, *rest = call(
            functools.partial(local_kernel, layer + 1),
            [all_columns, live] + [live] * (layer + 2 < layers),
            (state, delta, compact, ranks, volume_op, lift, trace),
            10**9,
        )
        kept = rest[0] if rest else None
    return pl.pallas_call(
        functools.partial(last_kernel, layers - 1),
        out_specs=pl.BlockSpec(memory_space=pltpu.MemorySpace.HBM),
        out_shape=jax.ShapeDtypeStruct((comps, elems), F32),
        scratch_shapes=[pltpu.VMEM((comps, elems), F32), pltpu.SemaphoreType.DMA],
        compiler_params=pltpu.CompilerParams(vmem_limit_bytes=VMEM),
    )(*received, compact, base, ranks, powers, lift, state)


def solution(mesh):
    both = ("wide", "narrow")
    return jax.shard_map(
        local,
        mesh=mesh,
        in_specs=(P(None, both), P(None, both), P(both), P(both), P(None, both), P(both), P(), P(), P()),
        out_specs=P(None, both),
        check_vma=False,
    )
```

```python
import jax
import jax.numpy as jnp
from jax import lax
from jax.experimental import pallas as pl
from jax.experimental.pallas import tpu as pltpu
from jax.sharding import PartitionSpec as P

TENT_SIZE = 16
MAX_TENTS = 24
MAX_LIVE = TENT_SIZE * MAX_TENTS
ROWS = 64
BLOCK = 256
SPLIT = 256
CHUNK = 512
LANES = 128
VMEM = 24 * 2**20
POWER_ROWS = 112
PHASES = (("wide", 1), ("narrow", 1), ("wide", 0), ("narrow", 0))
BF16, F32, I32 = jnp.bfloat16, jnp.float32, jnp.int32


def mm(left, right):
    return jnp.dot(left, right, preferred_element_type=F32)


def mm_t(left, right):
    return lax.dot_general(left, right, (((1,), (1,)), ((), ())), preferred_element_type=F32)


def low_of(index):
    return index & (BLOCK - 1)


def high_of(index):
    return index >> 8


def hot(index, depth):
    low, high = low_of(index), high_of(index)
    rows = lax.broadcasted_iota(I32, (BLOCK, index.shape[1]), 0).astype(F32).astype(BF16)
    parts = []
    for b in range(-(-depth // BLOCK)):
        here = jnp.where(high == b, low, -1).astype(F32).astype(BF16)
        count = min(BLOCK, depth - b * BLOCK)
        parts.append(jnp.where(rows[:count] == here, jnp.ones((), BF16), jnp.zeros((), BF16)))
    return parts[0] if len(parts) == 1 else jnp.concatenate(parts, axis=0)


def choose(found, key, first, rows, default=None):
    count = found.shape[0] // rows
    total = found[(count - 1) * rows :]
    if default is not None:
        total = jnp.where(key == first + count - 1, total, default)
    for b in range(count - 2, -1, -1):
        total = jnp.where(key == first + b, found[b * rows : (b + 1) * rows], total)
    return total


def stack(table):
    return jnp.concatenate([table[:, at : at + BLOCK] for at in range(0, table.shape[1], BLOCK)], axis=0)


def pick(table, low, high, first=0, default=0.0):
    return choose(mm(stack(table), hot(low, BLOCK)), high, first, table.shape[0], default)


def two_parts(values):
    rows = values.shape[0]
    start = -(-rows // 16) * 16
    top = values.astype(BF16).astype(F32)
    gap = jnp.zeros((start - rows, values.shape[1]), F32)
    return jnp.concatenate([jnp.concatenate([top, gap], axis=0), values - top], axis=0).astype(BF16), start


def three_parts(values):
    top = values.astype(BF16).astype(F32)
    mid = (values - top).astype(BF16).astype(F32)
    return top, mid, values - top - mid


def even(axis):
    return lax.axis_index(axis) % 2 == 0


def by_phase(columns):
    half, quarter = columns.shape[1] // 3, columns.shape[1] // 6
    low, high = columns[:, :half], columns[:, half : 2 * half]
    left, right = columns[:, 2 * half : 2 * half + quarter], columns[:, 2 * half + quarter :]
    wide, narrow = even("wide"), even("narrow")
    return jnp.concatenate(
        [
            jnp.where(wide, low, high),
            jnp.where(wide, high, low),
            jnp.where(narrow, left, right),
            jnp.where(narrow, right, left),
        ],
        axis=1,
    )


def remote_by_phase(near, local_columns, halo):
    half, quarter = halo // 3, halo // 6
    at = near - local_columns
    wide, narrow = even("wide"), even("narrow")
    in_wide = jnp.where(wide, at, jnp.where(at < half, at + half, at - half))
    in_narrow = jnp.where(narrow, at, jnp.where(at < 2 * half + quarter, at + quarter, at - quarter))
    return jnp.where(at < 0, near, local_columns + jnp.where(at < 2 * half, in_wide, in_narrow))


def store_blocks(out, refs):
    at = 0
    for ref in refs:
        width = ref.shape[1]
        ref[...] = out[:, at : at + width].astype(BF16)
        at += width


def row_of(ref):
    return jnp.concatenate([ref[i : i + 1, :] for i in range(ref.shape[0])], axis=1)


def face_rows(op, face):
    gap = jnp.zeros((ROWS - op.shape[0], op.shape[2]), F32)
    return jnp.concatenate([op[:, face, :].astype(F32), gap], axis=0)


def first_kernel(*refs):
    count = (len(refs) - 4) // 2
    inputs, blocks, held, sems = refs[:count], refs[count : count + 4], refs[count + 4 : -1], refs[-1]
    copies = [pltpu.make_async_copy(src, dst, sems.at[i]) for i, (src, dst) in enumerate(zip(inputs, held))]
    for copy in copies:
        copy.start()
    state, boundary, trace_op = held[:3]
    copies[1].wait()
    at = by_phase(row_of(boundary))
    chosen, high = hot(low_of(at), BLOCK), high_of(at)
    copies[2].wait()
    face = face_rows(trace_op, 3).astype(BF16)
    copies[0].wait()
    traces = mm(face, state[...].astype(BF16)).astype(BF16)
    store_blocks(choose(mm(stack(traces), chosen), high, 0, ROWS), blocks)
    for copy in copies[3:]:
        copy.wait()


def make_index(neighbours, elem_tent, boundary, active, height, compact, ranks, sent):
    tent = row_of(elem_tent)
    elems = tent.shape[1]
    tents = height.shape[1]
    layers = active.shape[0]
    act = active[...].astype(F32)
    top, mid, low = three_parts(height[...])
    row = lax.broadcasted_iota(I32, (2 * layers, tents), 0)
    high_rows = jnp.where(row == 0, top, jnp.where(row == 1, mid, jnp.where(row == 2, low, 0.0)))
    found = mm(jnp.concatenate([act, act, high_rows], axis=0).astype(BF16), hot(tent, tents))
    live, high_rows = found[: 2 * layers], found[2 * layers :]
    upto = jnp.where(
        lax.broadcasted_iota(I32, (LANES, LANES), 0) <= lax.broadcasted_iota(I32, (LANES, LANES), 1), 1.0, 0.0
    ).astype(BF16)
    chunks = [live[:, at : at + LANES] for at in range(0, elems, LANES)]
    counts = mm(jnp.concatenate(chunks, axis=0).astype(BF16), upto)
    offset = jnp.zeros((2 * layers, 1), F32)
    parts = []
    for c in range(len(chunks)):
        part = counts[c * 2 * layers : (c + 1) * 2 * layers]
        parts.append(part + offset)
        offset = offset + part[:, LANES - 1 :]
    place = jnp.where(live > 0.5, jnp.concatenate(parts, axis=1), 0.0).astype(I32)
    ranks[...] = place - 1
    row = lax.broadcasted_iota(I32, (2 * layers, elems), 0)
    digits = jnp.where(row < layers, low_of(place), high_of(place)).astype(F32)
    table = jnp.concatenate([digits, jnp.zeros_like(digits)], axis=0).astype(BF16)
    at = by_phase(row_of(boundary))
    found = pick(table, low_of(at), high_of(at))
    sent[...] = (found[:layers] + BLOCK * found[layers : 2 * layers]).astype(I32) - 1

    near = remote_by_phase(neighbours[...], 4 * elems, at.shape[1])
    near = jnp.concatenate([near, near], axis=0)
    near = jnp.where(row < layers, low_of(near), high_of(near)).astype(F32)
    elem = lax.broadcasted_iota(I32, (2 * layers, elems), 1)
    own = jnp.where(row == 3, low_of(elem).astype(F32), jnp.where(row == 4, high_of(elem).astype(F32), 0.0))
    rows16 = jnp.concatenate([near, high_rows + own], axis=0)
    count = MAX_LIVE // LANES
    for l in range(0, layers, 2):
        tables, columns = [], []
        for m in (l, l + 1):
            rank = place[m : m + 1] - 1
            tables += [jnp.where(rank >> 7 == b, rows16, 0.0) for b in range(count)]
            columns.append(hot(jnp.where(rank < 0, -1, rank & (LANES - 1)), LANES))
        found = mm_t(jnp.concatenate(tables, axis=0).astype(BF16), jnp.concatenate(columns, axis=0))
        for m in (0, 1):
            for b in range(count):
                at = 16 * (m * count + b)
                compact[l + m, :, b * LANES : (b + 1) * LANES] = found[at : at + 16, m * LANES : (m + 1) * LANES]
            compact[l + m, 13:14, :LANES] = jnp.broadcast_to(offset[l + m : l + m + 1], (1, LANES))


def whole(compact, row, count, here):
    rows = [compact[i : i + 1, here] for i in range(row, row + count)]
    return (rows[0] if count == 1 else jnp.concatenate(rows, axis=1)).astype(I32)


def many(compact):
    return jnp.max(compact[13:14, :LANES]) > SPLIT


FIRST, OTHERS = slice(0, SPLIT), slice(SPLIT, MAX_LIVE)


def by_face(columns):
    n = columns.shape[1] // 4
    return jnp.concatenate([columns[:, g * n : (g + 1) * n] for g in range(4)], axis=0)


def local_part(values, compact, here, volume, lift, trace, base, kept):
    comps, elems = values.shape
    blocks = elems // BLOCK
    count = here.stop - here.start
    parts, rows = two_parts(values)
    top = stack(parts[:rows])
    low = jnp.concatenate([whole(compact, 11, 1, here), whole(compact, 0, 4, here)], axis=1)
    high = jnp.concatenate([whole(compact, 12, 1, here), whole(compact, 4, 4, here)], axis=1)
    block, face = high & (blocks - 1), high // blocks
    near = []
    for at in range(0, low.shape[1], CHUNK):
        now = slice(at, at + CHUNK)
        near.append(choose(mm(top, hot(low[:, now], BLOCK)), block[:, now], 0, rows)[:comps].astype(BF16))
    near = jnp.concatenate(near, axis=1)
    mine, near, face = near[:, :count], near[:, count:], face[:, count:]
    picked = []
    for at in range(0, near.shape[1], CHUNK):
        now = slice(at, at + CHUNK)
        picked.append(choose(mm(trace[...], near[:, now]), face[:, now], 0, ROWS, 0.0))
    picked = by_face(jnp.concatenate(picked, axis=1)).astype(BF16)
    if kept is not None:
        rest = stack(jnp.concatenate([parts[rows:].astype(F32), jnp.zeros((rows - comps, elems), F32)], axis=0))
        rest = choose(mm(rest.astype(BF16), hot(low[:, :count], BLOCK)), block[:, :count], 0, rows)
        kept[:, here] = mine.astype(F32) + rest[:comps]
    base[:, here] = mm(volume[...], mine) + mm(lift[...], picked)


def local_parts(values, compact, *refs):
    local_part(values[...], compact, FIRST, *refs)

    @pl.when(many(compact))
    def _():
        local_part(values[...], compact, OTHERS, *refs)


def local_first_kernel(
    state, neighbours, elem_tent, boundary, active, height, volume, lift_op, trace_op,
    compact, ranks, sent, base, kept, lift, trace, powers,
):
    powers[...] = powers_of(volume[...])
    make_index(neighbours, elem_tent, boundary, active, height, compact, ranks, sent)
    lifts = jnp.concatenate([face_rows(lift_op, g) for g in range(4)], axis=0).astype(BF16)
    comps = lifts.shape[1]
    diagonal = lax.broadcasted_iota(I32, (comps, comps), 0) == lax.broadcasted_iota(I32, (comps, comps), 1)
    lift[...] = mm_t(jnp.where(diagonal, 1.0, 0.0).astype(BF16), lifts).astype(BF16)
    trace[...] = jnp.concatenate([face_rows(trace_op, g) for g in range(4)], axis=0).astype(BF16)
    local_parts(state, compact[0], volume, lift, trace, base, kept)


def scatter(delta, rank, here):
    parts, second = two_parts(delta)
    found = mm(parts, hot(rank - here.start, delta.shape[1]))
    return found[: delta.shape[0]] + found[second:]


def local_kernel(
    state, delta, compact, ranks, sent, volume, lift, trace, new_state, new_compact, new_ranks, new_sent, base, kept
):
    rank = ranks[0:1]
    more = many(compact[0])
    new_state[...] = state[...] + scatter(delta[:, FIRST], rank, FIRST)

    @pl.when(more)
    def _():
        new_state[...] = new_state[...] + scatter(delta[:, OTHERS], rank, OTHERS)

    tables = [compact[l] for l in range(1, compact.shape[0])]
    for l, table in enumerate(tables):
        new_compact[l] = table
    later_ranks, later_sent = ranks[1:], sent[1:]
    new_ranks[:-1, :] = later_ranks
    new_sent[:-1, :] = later_sent
    local_parts(new_state, tables[0], volume, lift, trace, base, kept)


def powers_of(volume):
    gap = jnp.zeros((POWER_ROWS - volume.shape[0], volume.shape[1]), F32)
    parts = [volume.astype(F32)]
    for _ in range(2):
        power = sum(mm(part.astype(BF16), volume) for part in parts[-2:])
        top = power.astype(BF16).astype(F32)
        parts += [top, power - top]
    return jnp.concatenate([half for part in parts for half in (part, gap)], axis=0).astype(BF16)


def taylor_terms(received, compact, here, base, powers, lift):
    remote = jnp.concatenate([ref[...] for ref in received], axis=1)
    first_block = 4 * 1024 // BLOCK
    picked = by_face(pick(remote, whole(compact, 0, 4, here), whole(compact, 4, 4, here), first_block)).astype(BF16)
    heights = compact[8:9, here] + compact[9:10, here] + compact[10:11, here]
    first = heights * (base[:, here] + mm(lift[...], picked))
    found = mm(powers[...], first.astype(BF16))
    comps = first.shape[0]
    products = [found[at : at + comps] for at in range(0, found.shape[0], POWER_ROWS)]
    total, scale = first, 1.0
    for order, product in ((2, products[0]), (3, products[1] + products[2]), (4, products[3] + products[4])):
        scale = scale * (heights / order)
        total = total + scale * product
    return total


def advance_kernel(r0, r1, r2, r3, o0, o1, o2, o3, compact, base, kept, sent, powers, lift, trace, delta, *outgoing):
    rows = compact[0]

    def part(here, before):
        place = sent[0:1] - here.start
        chosen = hot(place, here.stop - here.start)
        total = taylor_terms((r0, r1, r2, r3), rows, here, base, powers, lift)
        delta[:, here] = total
        traces = mm(trace[3 * ROWS :, :], (kept[:, here] + total).astype(BF16)).astype(BF16)
        before = jnp.concatenate([ref[...] for ref in before], axis=1).astype(F32)
        inside = jnp.logical_and(place >= 0, place < here.stop - here.start)
        store_blocks(jnp.where(inside, mm(traces, chosen), before), outgoing)

    part(FIRST, (o0, o1, o2, o3))

    @pl.when(many(rows))
    def _():
        part(OTHERS, outgoing)


def last_kernel(r0, r1, r2, r3, compact, base, ranks, powers, lift, state, advanced, held, sem):
    rows, rank = compact[0], ranks[0:1]

    def part(here, before):
        total = taylor_terms((r0, r1, r2, r3), rows, here, base, powers, lift)
        held[...] = before[...] + scatter(total, rank, here)

    part(FIRST, state)

    @pl.when(many(rows))
    def _():
        part(OTHERS, held)

    copy = pltpu.make_async_copy(held, advanced, sem)
    copy.start()
    copy.wait()


def call(kernel, outs, args, flops, aliases={}):
    outs = [jax.ShapeDtypeStruct(shape, dtype) for shape, dtype in outs]
    return pl.pallas_call(
        kernel,
        out_shape=outs,
        input_output_aliases=aliases,
        compiler_params=pltpu.CompilerParams(vmem_limit_bytes=VMEM),
        cost_estimate=pl.CostEstimate(flops=flops, bytes_accessed=2**20, transcendentals=0),
    )(*args)


def swapped(block, axis, first):
    pairs = [(i, i + 1) for i in range(first, lax.axis_size(axis) - 1, 2)]
    return lax.ppermute(block, axis, pairs + [(j, i) for i, j in pairs])


def exchange(outgoing):
    wide_1, wide_0, narrow_1, narrow_0 = outgoing
    wide_1, narrow_1, wide_0, narrow_0 = [
        swapped(block, axis, first)
        for block, (axis, first) in zip((wide_1, narrow_1, wide_0, narrow_0), PHASES)
    ]
    return wide_1, wide_0, narrow_1, narrow_0


def local(state, neighbours, elem_tent, boundary, active, tent_height, volume_op, lift_op, trace_op):
    comps, elems = state.shape
    layers = active.shape[0]
    halo = boundary.shape[0]
    wide_len = halo // 3
    narrow_len = wide_len // 2
    boundary = boundary.reshape(-1, LANES)
    elem_tent = elem_tent.reshape(-1, LANES)
    tent_height = tent_height.reshape(1, -1)

    blocks = [((ROWS, width), BF16) for width in (wide_len, wide_len, narrow_len, narrow_len)]
    live = ((comps, MAX_LIVE), F32)
    all_columns = ((comps, elems), F32)
    args = (
        state, boundary, trace_op.transpose(1, 0, 2), neighbours, elem_tent, active, tent_height, volume_op,
        lift_op.transpose(2, 0, 1),
    )
    held = [jax.ShapeDtypeStruct(arg.shape, arg.dtype) for arg in args]
    outs = pl.pallas_call(
        first_kernel,
        in_specs=[pl.BlockSpec(memory_space=pltpu.MemorySpace.HBM)] * len(args),
        out_shape=[jax.ShapeDtypeStruct(shape, dtype) for shape, dtype in blocks] + held,
        scratch_shapes=[pltpu.SemaphoreType.DMA((len(args),))],
        compiler_params=pltpu.CompilerParams(vmem_limit_bytes=VMEM),
    )(*[pltpu.with_memory_space_constraint(arg, pltpu.MemorySpace.HBM) for arg in args])
    outgoing = outs[:4]
    state, boundary, trace, neighbours, elem_tent, active, tent_height, volume_op, lift = outs[4:]
    received = exchange(outgoing)
    compact, ranks, sent, base, kept, lift, trace, powers = call(
        local_first_kernel,
        [
            ((layers, 16, MAX_LIVE), F32),
            ((2 * layers, elems), I32),
            ((layers, halo), I32),
            live,
            live,
            ((comps, 4 * ROWS), BF16),
            ((4 * ROWS, comps), BF16),
            ((5 * POWER_ROWS, comps), BF16),
        ],
        (state, neighbours, elem_tent, boundary, active, tent_height, volume_op, lift, trace),
        10**6,
    )
    tables = [(compact.shape, F32), (ranks.shape, I32), (sent.shape, I32)]

    def layer(_, carry):
        received, outgoing, state, compact, ranks, sent, base, kept = carry
        delta, *outgoing = call(
            advance_kernel,
            [live] + blocks,
            (*received, *outgoing, compact, base, kept, sent, powers, lift, trace),
            10**6,
            {4 + i: 1 + i for i in range(4)},
        )
        received = exchange(outgoing)
        state, compact, ranks, sent, base, kept = call(
            local_kernel,
            [all_columns, *tables, live, live],
            (state, delta, compact, ranks, sent, volume_op, lift, trace),
            10**6,
            {0: 0, 2: 1, 3: 2, 4: 3},
        )
        return received, tuple(outgoing), state, compact, ranks, sent, base, kept

    received, _, state, compact, ranks, _, base, _ = lax.fori_loop(
        0, layers - 1, layer, (received, tuple(outgoing), state, compact, ranks, sent, base, kept)
    )
    return pl.pallas_call(
        last_kernel,
        out_specs=pl.BlockSpec(memory_space=pltpu.MemorySpace.HBM),
        out_shape=jax.ShapeDtypeStruct((comps, elems), F32),
        scratch_shapes=[pltpu.VMEM((comps, elems), F32), pltpu.SemaphoreType.DMA],
        compiler_params=pltpu.CompilerParams(vmem_limit_bytes=VMEM),
    )(*received, compact, base, ranks, powers, lift, state)


def solution(mesh):
    both = ("wide", "narrow")
    return jax.shard_map(
        local,
        mesh=mesh,
        in_specs=(P(None, both), P(None, both), P(both), P(both), P(None, both), P(both), P(), P(), P()),
        out_specs=P(None, both),
        check_vma=False,
    )
```

```python
import jax
import jax.numpy as jnp
from jax import lax
from jax.experimental import pallas as pl
from jax.experimental.pallas import tpu as pltpu
from jax.sharding import PartitionSpec as P

TENT_SIZE = 16
MAX_TENTS = 24
MAX_LIVE = TENT_SIZE * MAX_TENTS
ROWS = 64
BLOCK = 256
SPLIT = 256
CHUNK = 512
LANES = 128
VMEM = 24 * 2**20
POWER_ROWS = 112
PHASES = (("wide", 1), ("narrow", 1), ("wide", 0), ("narrow", 0))
BF16, F32, I32 = jnp.bfloat16, jnp.float32, jnp.int32


def mm(left, right):
    return jnp.dot(left, right, preferred_element_type=F32)


def mm_t(left, right):
    return lax.dot_general(left, right, (((1,), (1,)), ((), ())), preferred_element_type=F32)


def low_of(index):
    return index & (BLOCK - 1)


def high_of(index):
    return index >> 8


def hot(index, depth):
    low, high = low_of(index), high_of(index)
    rows = lax.broadcasted_iota(I32, (BLOCK, index.shape[1]), 0).astype(F32).astype(BF16)
    parts = []
    for b in range(-(-depth // BLOCK)):
        here = jnp.where(high == b, low, -1).astype(F32).astype(BF16)
        count = min(BLOCK, depth - b * BLOCK)
        parts.append(jnp.where(rows[:count] == here, jnp.ones((), BF16), jnp.zeros((), BF16)))
    return parts[0] if len(parts) == 1 else jnp.concatenate(parts, axis=0)


def choose(found, key, first, rows, default=None):
    count = found.shape[0] // rows
    total = found[(count - 1) * rows :]
    if default is not None:
        total = jnp.where(key == first + count - 1, total, default)
    for b in range(count - 2, -1, -1):
        total = jnp.where(key == first + b, found[b * rows : (b + 1) * rows], total)
    return total


def stack(table):
    return jnp.concatenate([table[:, at : at + BLOCK] for at in range(0, table.shape[1], BLOCK)], axis=0)


def pick(table, low, high, first=0, default=0.0):
    return choose(mm(stack(table), hot(low, BLOCK)), high, first, table.shape[0], default)


def two_parts(values):
    rows = values.shape[0]
    start = -(-rows // 16) * 16
    top = values.astype(BF16).astype(F32)
    gap = jnp.zeros((start - rows, values.shape[1]), F32)
    return jnp.concatenate([jnp.concatenate([top, gap], axis=0), values - top], axis=0).astype(BF16), start


def three_parts(values):
    top = values.astype(BF16).astype(F32)
    mid = (values - top).astype(BF16).astype(F32)
    return top, mid, values - top - mid


def even(axis):
    return lax.axis_index(axis) % 2 == 0


def by_phase(columns):
    half, quarter = columns.shape[1] // 3, columns.shape[1] // 6
    low, high = columns[:, :half], columns[:, half : 2 * half]
    left, right = columns[:, 2 * half : 2 * half + quarter], columns[:, 2 * half + quarter :]
    wide, narrow = even("wide"), even("narrow")
    return jnp.concatenate(
        [
            jnp.where(wide, low, high),
            jnp.where(wide, high, low),
            jnp.where(narrow, left, right),
            jnp.where(narrow, right, left),
        ],
        axis=1,
    )


def remote_by_phase(near, local_columns, halo):
    half, quarter = halo // 3, halo // 6
    at = near - local_columns
    wide, narrow = even("wide"), even("narrow")
    in_wide = jnp.where(wide, at, jnp.where(at < half, at + half, at - half))
    in_narrow = jnp.where(narrow, at, jnp.where(at < 2 * half + quarter, at + quarter, at - quarter))
    return jnp.where(at < 0, near, local_columns + jnp.where(at < 2 * half, in_wide, in_narrow))


def store_blocks(out, refs):
    at = 0
    for ref in refs:
        width = ref.shape[1]
        ref[...] = out[:, at : at + width].astype(BF16)
        at += width


def row_of(ref):
    return jnp.concatenate([ref[i : i + 1, :] for i in range(ref.shape[0])], axis=1)


def face_rows(op, face):
    gap = jnp.zeros((ROWS - op.shape[0], op.shape[2]), F32)
    return jnp.concatenate([op[:, face, :].astype(F32), gap], axis=0)


def first_kernel(*refs):
    count = (len(refs) - 4) // 2
    inputs, blocks, held, sems = refs[:count], refs[count : count + 4], refs[count + 4 : -1], refs[-1]
    copies = [pltpu.make_async_copy(src, dst, sems.at[i]) for i, (src, dst) in enumerate(zip(inputs, held))]
    for copy in copies:
        copy.start()
    state, boundary, trace_op = held[:3]
    copies[1].wait()
    at = by_phase(row_of(boundary))
    chosen, high = hot(low_of(at), BLOCK), high_of(at)
    copies[2].wait()
    face = face_rows(trace_op, 3).astype(BF16)
    copies[0].wait()
    traces = mm(face, state[...].astype(BF16)).astype(BF16)
    store_blocks(choose(mm(stack(traces), chosen), high, 0, ROWS), blocks)
    for copy in copies[3:]:
        copy.wait()


def make_index(neighbours, elem_tent, boundary, active, height, compact, ranks, sent):
    tent = row_of(elem_tent)
    elems = tent.shape[1]
    tents = height.shape[1]
    layers = active.shape[0]
    act = active[...].astype(F32)
    top, mid, low = three_parts(height[...])
    row = lax.broadcasted_iota(I32, (2 * layers, tents), 0)
    high_rows = jnp.where(row == 0, top, jnp.where(row == 1, mid, jnp.where(row == 2, low, 0.0)))
    found = mm(jnp.concatenate([act, act, high_rows], axis=0).astype(BF16), hot(tent, tents))
    live, high_rows = found[: 2 * layers], found[2 * layers :]
    upto = jnp.where(
        lax.broadcasted_iota(I32, (LANES, LANES), 0) <= lax.broadcasted_iota(I32, (LANES, LANES), 1), 1.0, 0.0
    ).astype(BF16)
    chunks = [live[:, at : at + LANES] for at in range(0, elems, LANES)]
    counts = mm(jnp.concatenate(chunks, axis=0).astype(BF16), upto)
    offset = jnp.zeros((2 * layers, 1), F32)
    parts = []
    for c in range(len(chunks)):
        part = counts[c * 2 * layers : (c + 1) * 2 * layers]
        parts.append(part + offset)
        offset = offset + part[:, LANES - 1 :]
    place = jnp.where(live > 0.5, jnp.concatenate(parts, axis=1), 0.0).astype(I32)
    ranks[...] = place - 1
    row = lax.broadcasted_iota(I32, (2 * layers, elems), 0)
    digits = jnp.where(row < layers, low_of(place), high_of(place)).astype(F32)
    table = jnp.concatenate([digits, jnp.zeros_like(digits)], axis=0).astype(BF16)
    at = by_phase(row_of(boundary))
    found = pick(table, low_of(at), high_of(at))
    sent[...] = (found[:layers] + BLOCK * found[layers : 2 * layers]).astype(I32) - 1

    near = remote_by_phase(neighbours[...], 4 * elems, at.shape[1])
    near = jnp.concatenate([near, near], axis=0)
    near = jnp.where(row < layers, low_of(near), high_of(near)).astype(F32)
    elem = lax.broadcasted_iota(I32, (2 * layers, elems), 1)
    own = jnp.where(row == 3, low_of(elem).astype(F32), jnp.where(row == 4, high_of(elem).astype(F32), 0.0))
    rows16 = jnp.concatenate([near, high_rows + own], axis=0)
    count = MAX_LIVE // LANES
    for l in range(0, layers, 2):
        tables, columns = [], []
        for m in (l, l + 1):
            rank = place[m : m + 1] - 1
            tables += [jnp.where(rank >> 7 == b, rows16, 0.0) for b in range(count)]
            columns.append(hot(jnp.where(rank < 0, -1, rank & (LANES - 1)), LANES))
        found = mm_t(jnp.concatenate(tables, axis=0).astype(BF16), jnp.concatenate(columns, axis=0))
        for m in (0, 1):
            for b in range(count):
                at = 16 * (m * count + b)
                compact[l + m, :, b * LANES : (b + 1) * LANES] = found[at : at + 16, m * LANES : (m + 1) * LANES]
            compact[l + m, 13:14, :LANES] = jnp.broadcast_to(offset[l + m : l + m + 1], (1, LANES))


def whole(compact, row, count, here):
    rows = [compact[i : i + 1, here] for i in range(row, row + count)]
    return (rows[0] if count == 1 else jnp.concatenate(rows, axis=1)).astype(I32)


def many(compact):
    return jnp.max(compact[13:14, :LANES]) > SPLIT


FIRST, OTHERS = slice(0, SPLIT), slice(SPLIT, MAX_LIVE)


def by_face(columns):
    n = columns.shape[1] // 4
    return jnp.concatenate([columns[:, g * n : (g + 1) * n] for g in range(4)], axis=0)


def local_part(values, compact, here, volume, lift, trace, base, kept):
    comps, elems = values.shape
    blocks = elems // BLOCK
    count = here.stop - here.start
    parts, rows = two_parts(values)
    top = stack(parts[:rows])
    low = jnp.concatenate([whole(compact, 11, 1, here), whole(compact, 0, 4, here)], axis=1)
    high = jnp.concatenate([whole(compact, 12, 1, here), whole(compact, 4, 4, here)], axis=1)
    block, face = high & (blocks - 1), high // blocks
    near = []
    for at in range(0, low.shape[1], CHUNK):
        now = slice(at, at + CHUNK)
        near.append(choose(mm(top, hot(low[:, now], BLOCK)), block[:, now], 0, rows)[:comps].astype(BF16))
    near = jnp.concatenate(near, axis=1)
    mine, near, face = near[:, :count], near[:, count:], face[:, count:]
    picked = []
    for at in range(0, near.shape[1], CHUNK):
        now = slice(at, at + CHUNK)
        picked.append(choose(mm(trace[...], near[:, now]), face[:, now], 0, ROWS, 0.0))
    picked = by_face(jnp.concatenate(picked, axis=1)).astype(BF16)
    if kept is not None:
        rest = stack(jnp.concatenate([parts[rows:].astype(F32), jnp.zeros((rows - comps, elems), F32)], axis=0))
        rest = choose(mm(rest.astype(BF16), hot(low[:, :count], BLOCK)), block[:, :count], 0, rows)
        kept[:, here] = mine.astype(F32) + rest[:comps]
    base[:, here] = mm(volume[...], mine) + mm(lift[...], picked)


def local_parts(values, state, compact, *refs):
    local_part(values, compact, FIRST, *refs)

    @pl.when(many(compact))
    def _():
        local_part(state[...], compact, OTHERS, *refs)


def local_first_kernel(
    state, neighbours, elem_tent, boundary, active, height, volume, lift_op, trace_op,
    compact, ranks, sent, base, kept, lift, trace, powers,
):
    powers[...] = powers_of(volume[...])
    make_index(neighbours, elem_tent, boundary, active, height, compact, ranks, sent)
    lifts = jnp.concatenate([face_rows(lift_op, g) for g in range(4)], axis=0).astype(BF16)
    comps = lifts.shape[1]
    diagonal = lax.broadcasted_iota(I32, (comps, comps), 0) == lax.broadcasted_iota(I32, (comps, comps), 1)
    lift[...] = mm_t(jnp.where(diagonal, 1.0, 0.0).astype(BF16), lifts).astype(BF16)
    trace[...] = jnp.concatenate([face_rows(trace_op, g) for g in range(4)], axis=0).astype(BF16)
    local_parts(state[...], state, compact[0], volume, lift, trace, base, kept)


def scatter(delta, rank, here):
    parts, second = two_parts(delta)
    found = mm(parts, hot(rank - here.start, delta.shape[1]))
    return found[: delta.shape[0]] + found[second:]


def local_kernel(
    state, delta, compact, ranks, sent, volume, lift, trace, new_state, new_compact, new_ranks, new_sent, base, kept
):
    values = state[...] + scatter(delta[...], ranks[0:1], FIRST)
    new_state[...] = values
    tables = [compact[l] for l in range(1, compact.shape[0])]
    for l, table in enumerate(tables):
        new_compact[l] = table
    later_ranks, later_sent = ranks[1:], sent[1:]
    new_ranks[:-1, :] = later_ranks
    new_sent[:-1, :] = later_sent
    local_parts(values, new_state, tables[0], volume, lift, trace, base, kept)


def powers_of(volume):
    gap = jnp.zeros((POWER_ROWS - volume.shape[0], volume.shape[1]), F32)
    parts = [volume.astype(F32)]
    for _ in range(2):
        power = sum(mm(part.astype(BF16), volume) for part in parts[-2:])
        top = power.astype(BF16).astype(F32)
        parts += [top, power - top]
    return jnp.concatenate([half for part in parts for half in (part, gap)], axis=0).astype(BF16)


def taylor_terms(received, compact, here, base, powers, lift):
    remote = jnp.concatenate([ref[...] for ref in received], axis=1)
    first_block = 4 * 1024 // BLOCK
    picked = by_face(pick(remote, whole(compact, 0, 4, here), whole(compact, 4, 4, here), first_block)).astype(BF16)
    heights = compact[8:9, here] + compact[9:10, here] + compact[10:11, here]
    first = heights * (base[:, here] + mm(lift[...], picked))
    found = mm(powers[...], first.astype(BF16))
    comps = first.shape[0]
    products = [found[at : at + comps] for at in range(0, found.shape[0], POWER_ROWS)]
    total, scale = first, 1.0
    for order, product in ((2, products[0]), (3, products[1] + products[2]), (4, products[3] + products[4])):
        scale = scale * (heights / order)
        total = total + scale * product
    return total


def advance_kernel(
    r0, r1, r2, r3, o0, o1, o2, o3, state, compact, base, kept, sent, ranks, powers, lift, trace,
    delta, out_0, out_1, out_2, out_3, new_state,
):
    rows = compact[0]
    outgoing = (out_0, out_1, out_2, out_3)

    def part(here, before):
        place = sent[0:1] - here.start
        chosen = hot(place, here.stop - here.start)
        total = taylor_terms((r0, r1, r2, r3), rows, here, base, powers, lift)
        traces = mm(trace[3 * ROWS :, :], (kept[:, here] + total).astype(BF16)).astype(BF16)
        before = jnp.concatenate([ref[...] for ref in before], axis=1).astype(F32)
        inside = jnp.logical_and(place >= 0, place < here.stop - here.start)
        store_blocks(jnp.where(inside, mm(traces, chosen), before), outgoing)
        return total

    new_state[...] = state[...]
    delta[...] = part(FIRST, (o0, o1, o2, o3))

    @pl.when(many(rows))
    def _():
        new_state[...] = new_state[...] + scatter(part(OTHERS, outgoing), ranks[0:1], OTHERS)


def last_kernel(r0, r1, r2, r3, compact, base, ranks, powers, lift, state, advanced, held, sem):
    rows, rank = compact[0], ranks[0:1]

    def part(here, before):
        total = taylor_terms((r0, r1, r2, r3), rows, here, base, powers, lift)
        held[...] = before[...] + scatter(total, rank, here)

    part(FIRST, state)

    @pl.when(many(rows))
    def _():
        part(OTHERS, held)

    copy = pltpu.make_async_copy(held, advanced, sem)
    copy.start()
    copy.wait()


def call(kernel, outs, args, flops, aliases={}):
    outs = [jax.ShapeDtypeStruct(shape, dtype) for shape, dtype in outs]
    return pl.pallas_call(
        kernel,
        out_shape=outs,
        input_output_aliases=aliases,
        compiler_params=pltpu.CompilerParams(vmem_limit_bytes=VMEM),
        cost_estimate=pl.CostEstimate(flops=flops, bytes_accessed=2**20, transcendentals=0),
    )(*args)


def swapped(block, axis, first):
    pairs = [(i, i + 1) for i in range(first, lax.axis_size(axis) - 1, 2)]
    return lax.ppermute(block, axis, pairs + [(j, i) for i, j in pairs])


def exchange(outgoing):
    wide_1, wide_0, narrow_1, narrow_0 = outgoing
    wide_1, narrow_1, wide_0, narrow_0 = [
        swapped(block, axis, first)
        for block, (axis, first) in zip((wide_1, narrow_1, wide_0, narrow_0), PHASES)
    ]
    return wide_1, wide_0, narrow_1, narrow_0


def local(state, neighbours, elem_tent, boundary, active, tent_height, volume_op, lift_op, trace_op):
    comps, elems = state.shape
    layers = active.shape[0]
    halo = boundary.shape[0]
    wide_len = halo // 3
    narrow_len = wide_len // 2
    boundary = boundary.reshape(-1, LANES)
    elem_tent = elem_tent.reshape(-1, LANES)
    tent_height = tent_height.reshape(1, -1)

    blocks = [((ROWS, width), BF16) for width in (wide_len, wide_len, narrow_len, narrow_len)]
    live = ((comps, MAX_LIVE), F32)
    all_columns = ((comps, elems), F32)
    args = (
        state, boundary, trace_op.transpose(1, 0, 2), neighbours, elem_tent, active, tent_height, volume_op,
        lift_op.transpose(2, 0, 1),
    )
    held = [jax.ShapeDtypeStruct(arg.shape, arg.dtype) for arg in args]
    outs = pl.pallas_call(
        first_kernel,
        in_specs=[pl.BlockSpec(memory_space=pltpu.MemorySpace.HBM)] * len(args),
        out_shape=[jax.ShapeDtypeStruct(shape, dtype) for shape, dtype in blocks] + held,
        scratch_shapes=[pltpu.SemaphoreType.DMA((len(args),))],
        compiler_params=pltpu.CompilerParams(vmem_limit_bytes=VMEM),
    )(*[pltpu.with_memory_space_constraint(arg, pltpu.MemorySpace.HBM) for arg in args])
    outgoing = outs[:4]
    state, boundary, trace, neighbours, elem_tent, active, tent_height, volume_op, lift = outs[4:]
    received = exchange(outgoing)
    compact, ranks, sent, base, kept, lift, trace, powers = call(
        local_first_kernel,
        [
            ((layers, 16, MAX_LIVE), F32),
            ((2 * layers, elems), I32),
            ((layers, halo), I32),
            live,
            live,
            ((comps, 4 * ROWS), BF16),
            ((4 * ROWS, comps), BF16),
            ((5 * POWER_ROWS, comps), BF16),
        ],
        (state, neighbours, elem_tent, boundary, active, tent_height, volume_op, lift, trace),
        10**6,
    )
    tables = [(compact.shape, F32), (ranks.shape, I32), (sent.shape, I32)]

    def layer(_, carry):
        received, outgoing, state, compact, ranks, sent, base, kept = carry
        delta, *outgoing, state = call(
            advance_kernel,
            [((comps, SPLIT), F32)] + blocks + [all_columns],
            (*received, *outgoing, state, compact, base, kept, sent, ranks, powers, lift, trace),
            10**6,
            {4 + i: 1 + i for i in range(5)},
        )
        received = exchange(outgoing)
        state, compact, ranks, sent, base, kept = call(
            local_kernel,
            [all_columns, *tables, live, live],
            (state, delta, compact, ranks, sent, volume_op, lift, trace),
            10**6,
            {0: 0, 2: 1, 3: 2, 4: 3},
        )
        return received, tuple(outgoing), state, compact, ranks, sent, base, kept

    received, _, state, compact, ranks, _, base, _ = lax.fori_loop(
        0, layers - 1, layer, (received, tuple(outgoing), state, compact, ranks, sent, base, kept)
    )
    return pl.pallas_call(
        last_kernel,
        out_specs=pl.BlockSpec(memory_space=pltpu.MemorySpace.HBM),
        out_shape=jax.ShapeDtypeStruct((comps, elems), F32),
        scratch_shapes=[pltpu.VMEM((comps, elems), F32), pltpu.SemaphoreType.DMA],
        compiler_params=pltpu.CompilerParams(vmem_limit_bytes=VMEM),
    )(*received, compact, base, ranks, powers, lift, state)


def solution(mesh):
    both = ("wide", "narrow")
    return jax.shard_map(
        local,
        mesh=mesh,
        in_specs=(P(None, both), P(None, both), P(both), P(both), P(None, both), P(both), P(), P(), P()),
        out_specs=P(None, both),
        check_vma=False,
    )
```

```python
import jax
import jax.numpy as jnp
from jax import lax
from jax.experimental import pallas as pl
from jax.experimental.pallas import tpu as pltpu
from jax.sharding import PartitionSpec as P

TENT_SIZE = 16
MAX_TENTS = 24
MAX_LIVE = TENT_SIZE * MAX_TENTS
ROWS = 64
BLOCK = 256
SPLIT = 256
CHUNK = 512
LANES = 128
VMEM = 24 * 2**20
POWER_ROWS = 112
PHASES = (("wide", 1), ("narrow", 1), ("wide", 0), ("narrow", 0))
BF16, F32, I32 = jnp.bfloat16, jnp.float32, jnp.int32


def mm(left, right):
    return jnp.dot(left, right, preferred_element_type=F32)


def mm_t(left, right):
    return lax.dot_general(left, right, (((1,), (1,)), ((), ())), preferred_element_type=F32)


def low_of(index):
    return index & (BLOCK - 1)


def high_of(index):
    return index >> 8


def hot(index, depth):
    low, high = low_of(index), high_of(index)
    rows = lax.broadcasted_iota(I32, (BLOCK, index.shape[1]), 0).astype(F32).astype(BF16)
    parts = []
    for b in range(-(-depth // BLOCK)):
        here = jnp.where(high == b, low, -1).astype(F32).astype(BF16)
        count = min(BLOCK, depth - b * BLOCK)
        parts.append(jnp.where(rows[:count] == here, jnp.ones((), BF16), jnp.zeros((), BF16)))
    return parts[0] if len(parts) == 1 else jnp.concatenate(parts, axis=0)


def choose(found, key, first, rows, default=None):
    count = found.shape[0] // rows
    total = found[(count - 1) * rows :]
    if default is not None:
        total = jnp.where(key == first + count - 1, total, default)
    for b in range(count - 2, -1, -1):
        total = jnp.where(key == first + b, found[b * rows : (b + 1) * rows], total)
    return total


def stack(table):
    return jnp.concatenate([table[:, at : at + BLOCK] for at in range(0, table.shape[1], BLOCK)], axis=0)


def pick(table, low, high, first=0, default=0.0):
    return choose(mm(stack(table), hot(low, BLOCK)), high, first, table.shape[0], default)


def two_parts(values):
    rows = values.shape[0]
    start = -(-rows // 16) * 16
    top = values.astype(BF16).astype(F32)
    gap = jnp.zeros((start - rows, values.shape[1]), F32)
    return jnp.concatenate([jnp.concatenate([top, gap], axis=0), values - top], axis=0).astype(BF16), start


def three_parts(values):
    top = values.astype(BF16).astype(F32)
    mid = (values - top).astype(BF16).astype(F32)
    return top, mid, values - top - mid


def even(axis):
    return lax.axis_index(axis) % 2 == 0


def by_phase(columns):
    half, quarter = columns.shape[1] // 3, columns.shape[1] // 6
    low, high = columns[:, :half], columns[:, half : 2 * half]
    left, right = columns[:, 2 * half : 2 * half + quarter], columns[:, 2 * half + quarter :]
    wide, narrow = even("wide"), even("narrow")
    return jnp.concatenate(
        [
            jnp.where(wide, low, high),
            jnp.where(wide, high, low),
            jnp.where(narrow, left, right),
            jnp.where(narrow, right, left),
        ],
        axis=1,
    )


def remote_by_phase(near, local_columns, halo):
    half, quarter = halo // 3, halo // 6
    at = near - local_columns
    wide, narrow = even("wide"), even("narrow")
    in_wide = jnp.where(wide, at, jnp.where(at < half, at + half, at - half))
    in_narrow = jnp.where(narrow, at, jnp.where(at < 2 * half + quarter, at + quarter, at - quarter))
    return jnp.where(at < 0, near, local_columns + jnp.where(at < 2 * half, in_wide, in_narrow))


def store_blocks(out, refs):
    at = 0
    for ref in refs:
        width = ref.shape[1]
        ref[...] = out[:, at : at + width].astype(BF16)
        at += width


def row_of(ref):
    return jnp.concatenate([ref[i : i + 1, :] for i in range(ref.shape[0])], axis=1)


def face_rows(op, face):
    gap = jnp.zeros((ROWS - op.shape[0], op.shape[2]), F32)
    return jnp.concatenate([op[:, face, :].astype(F32), gap], axis=0)


def first_kernel(*refs):
    count = (len(refs) - 4) // 2
    inputs, blocks, held, sems = refs[:count], refs[count : count + 4], refs[count + 4 : -1], refs[-1]
    copies = [pltpu.make_async_copy(src, dst, sems.at[i]) for i, (src, dst) in enumerate(zip(inputs, held))]
    for copy in copies:
        copy.start()
    state, boundary, trace_op = held[:3]
    copies[1].wait()
    at = by_phase(row_of(boundary))
    chosen, high = hot(low_of(at), BLOCK), high_of(at)
    copies[2].wait()
    face = face_rows(trace_op, 3).astype(BF16)
    copies[0].wait()
    traces = mm(face, state[...].astype(BF16)).astype(BF16)
    store_blocks(choose(mm(stack(traces), chosen), high, 0, ROWS), blocks)
    for copy in copies[3:]:
        copy.wait()


def make_index(neighbours, elem_tent, boundary, active, height, compact, ranks, sent):
    tent = row_of(elem_tent)
    elems = tent.shape[1]
    tents = height.shape[1]
    layers = active.shape[0]
    act = active[...].astype(F32)
    top, mid, low = three_parts(height[...])
    row = lax.broadcasted_iota(I32, (2 * layers, tents), 0)
    high_rows = jnp.where(row == 0, top, jnp.where(row == 1, mid, jnp.where(row == 2, low, 0.0)))
    found = mm(jnp.concatenate([act, act, high_rows], axis=0).astype(BF16), hot(tent, tents))
    live, high_rows = found[: 2 * layers], found[2 * layers :]
    upto = jnp.where(
        lax.broadcasted_iota(I32, (LANES, LANES), 0) <= lax.broadcasted_iota(I32, (LANES, LANES), 1), 1.0, 0.0
    ).astype(BF16)
    chunks = [live[:, at : at + LANES] for at in range(0, elems, LANES)]
    counts = mm(jnp.concatenate(chunks, axis=0).astype(BF16), upto)
    offset = jnp.zeros((2 * layers, 1), F32)
    parts = []
    for c in range(len(chunks)):
        part = counts[c * 2 * layers : (c + 1) * 2 * layers]
        parts.append(part + offset)
        offset = offset + part[:, LANES - 1 :]
    place = jnp.where(live > 0.5, jnp.concatenate(parts, axis=1), 0.0).astype(I32)
    ranks[...] = place - 1
    row = lax.broadcasted_iota(I32, (2 * layers, elems), 0)
    digits = jnp.where(row < layers, low_of(place), high_of(place)).astype(F32)
    table = jnp.concatenate([digits, jnp.zeros_like(digits)], axis=0).astype(BF16)
    at = by_phase(row_of(boundary))
    found = pick(table, low_of(at), high_of(at))
    sent[...] = (found[:layers] + BLOCK * found[layers : 2 * layers]).astype(I32) - 1

    near = remote_by_phase(neighbours[...], 4 * elems, at.shape[1])
    near = jnp.concatenate([near, near], axis=0)
    near = jnp.where(row < layers, low_of(near), high_of(near)).astype(F32)
    elem = lax.broadcasted_iota(I32, (2 * layers, elems), 1)
    own = jnp.where(row == 3, low_of(elem).astype(F32), jnp.where(row == 4, high_of(elem).astype(F32), 0.0))
    rows16 = jnp.concatenate([near, high_rows + own], axis=0)
    count = MAX_LIVE // LANES
    for l in range(0, layers, 2):
        tables, columns = [], []
        for m in (l, l + 1):
            rank = place[m : m + 1] - 1
            tables += [jnp.where(rank >> 7 == b, rows16, 0.0) for b in range(count)]
            columns.append(hot(jnp.where(rank < 0, -1, rank & (LANES - 1)), LANES))
        found = mm_t(jnp.concatenate(tables, axis=0).astype(BF16), jnp.concatenate(columns, axis=0))
        for m in (0, 1):
            for b in range(count):
                at = 16 * (m * count + b)
                compact[l + m, :, b * LANES : (b + 1) * LANES] = found[at : at + 16, m * LANES : (m + 1) * LANES]
            compact[l + m, 13:14, :LANES] = jnp.broadcast_to(offset[l + m : l + m + 1], (1, LANES))


def whole(compact, row, count, here):
    rows = [compact[i : i + 1, here] for i in range(row, row + count)]
    return (rows[0] if count == 1 else jnp.concatenate(rows, axis=1)).astype(I32)


def many(compact):
    return jnp.max(compact[13:14, :LANES]) > SPLIT


FIRST, OTHERS = slice(0, SPLIT), slice(SPLIT, MAX_LIVE)
ALL = slice(0, MAX_LIVE)


def by_face(columns):
    n = columns.shape[1] // 4
    return jnp.concatenate([columns[:, g * n : (g + 1) * n] for g in range(4)], axis=0)


def local_part(values, compact, here, volume, lift, trace, base, kept):
    comps, elems = values.shape
    blocks = elems // BLOCK
    count = here.stop - here.start
    parts, rows = two_parts(values)
    top = stack(parts[:rows])
    low = jnp.concatenate([whole(compact, 11, 1, here), whole(compact, 0, 4, here)], axis=1)
    high = jnp.concatenate([whole(compact, 12, 1, here), whole(compact, 4, 4, here)], axis=1)
    block, face = high & (blocks - 1), high // blocks
    near = []
    for at in range(0, low.shape[1], CHUNK):
        now = slice(at, at + CHUNK)
        near.append(choose(mm(top, hot(low[:, now], BLOCK)), block[:, now], 0, rows)[:comps].astype(BF16))
    near = jnp.concatenate(near, axis=1)
    mine, near, face = near[:, :count], near[:, count:], face[:, count:]
    picked = []
    for at in range(0, near.shape[1], CHUNK):
        now = slice(at, at + CHUNK)
        picked.append(choose(mm(trace[...], near[:, now]), face[:, now], 0, ROWS, 0.0))
    picked = by_face(jnp.concatenate(picked, axis=1)).astype(BF16)
    if kept is not None:
        rest = stack(jnp.concatenate([parts[rows:].astype(F32), jnp.zeros((rows - comps, elems), F32)], axis=0))
        rest = choose(mm(rest.astype(BF16), hot(low[:, :count], BLOCK)), block[:, :count], 0, rows)
        kept[:, here] = mine.astype(F32) + rest[:comps]
    base[:, here] = mm(volume[...], mine) + mm(lift[...], picked)


def local_parts(values, state, compact, *refs):
    local_part(values, compact, FIRST, *refs)
    for ref in refs[3:]:
        ref[:, OTHERS] = jnp.zeros((ref.shape[0], MAX_LIVE - SPLIT), F32)

    @pl.when(many(compact))
    def _():
        local_part(state[...], compact, OTHERS, *refs)


def local_first_kernel(
    state, neighbours, elem_tent, boundary, active, height, volume, lift_op, trace_op,
    compact, ranks, sent, base, kept, lift, trace, powers,
):
    powers[...] = powers_of(volume[...])
    make_index(neighbours, elem_tent, boundary, active, height, compact, ranks, sent)
    lifts = jnp.concatenate([face_rows(lift_op, g) for g in range(4)], axis=0).astype(BF16)
    comps = lifts.shape[1]
    diagonal = lax.broadcasted_iota(I32, (comps, comps), 0) == lax.broadcasted_iota(I32, (comps, comps), 1)
    lift[...] = mm_t(jnp.where(diagonal, 1.0, 0.0).astype(BF16), lifts).astype(BF16)
    trace[...] = jnp.concatenate([face_rows(trace_op, g) for g in range(4)], axis=0).astype(BF16)
    local_parts(state[...], state, compact[0], volume, lift, trace, base, kept)


def scatter(delta, rank):
    parts, second = two_parts(delta)
    found = mm(parts, hot(rank, MAX_LIVE))
    return found[: delta.shape[0]] + found[second:]


def local_kernel(
    state, delta, compact, ranks, sent, volume, lift, trace, new_state, new_compact, new_ranks, new_sent, base, kept
):
    values = state[...] + scatter(delta[...], ranks[0:1])
    new_state[...] = values
    tables = [compact[l] for l in range(1, compact.shape[0])]
    for l, table in enumerate(tables):
        new_compact[l] = table
    later_ranks, later_sent = ranks[1:], sent[1:]
    new_ranks[:-1, :] = later_ranks
    new_sent[:-1, :] = later_sent
    local_parts(values, new_state, tables[0], volume, lift, trace, base, kept)


def powers_of(volume):
    gap = jnp.zeros((POWER_ROWS - volume.shape[0], volume.shape[1]), F32)
    parts = [volume.astype(F32)]
    for _ in range(2):
        power = sum(mm(part.astype(BF16), volume) for part in parts[-2:])
        top = power.astype(BF16).astype(F32)
        parts += [top, power - top]
    return jnp.concatenate([half for part in parts for half in (part, gap)], axis=0).astype(BF16)


def taylor_terms(received, compact, here, base, powers, lift):
    remote = jnp.concatenate([ref[...] for ref in received], axis=1)
    first_block = 4 * 1024 // BLOCK
    picked = by_face(pick(remote, whole(compact, 0, 4, here), whole(compact, 4, 4, here), first_block)).astype(BF16)
    heights = compact[8:9, here] + compact[9:10, here] + compact[10:11, here]
    first = heights * (base[:, here] + mm(lift[...], picked))
    found = mm(powers[...], first.astype(BF16))
    comps = first.shape[0]
    products = [found[at : at + comps] for at in range(0, found.shape[0], POWER_ROWS)]
    total, scale = first, 1.0
    for order, product in ((2, products[0]), (3, products[1] + products[2]), (4, products[3] + products[4])):
        scale = scale * (heights / order)
        total = total + scale * product
    return total


def advance_kernel(r0, r1, r2, r3, o0, o1, o2, o3, compact, base, kept, sent, powers, lift, trace, delta, *outgoing):
    place = sent[0:1]
    chosen, high = hot(low_of(place), BLOCK), high_of(place)
    total = taylor_terms((r0, r1, r2, r3), compact[0], ALL, base, powers, lift)
    delta[...] = total
    traces = mm(trace[3 * ROWS :, :], (kept[...] + total).astype(BF16))
    rest = -MAX_LIVE % BLOCK
    table = jnp.concatenate([traces, jnp.zeros((ROWS, rest), F32)], axis=1).astype(BF16)
    before = jnp.concatenate([o0[...], o1[...], o2[...], o3[...]], axis=1).astype(F32)
    store_blocks(choose(mm(stack(table), chosen), high, 0, ROWS, before), outgoing)


def last_kernel(r0, r1, r2, r3, compact, base, ranks, powers, lift, state, advanced, held, sem):
    total = taylor_terms((r0, r1, r2, r3), compact[0], ALL, base, powers, lift)
    held[...] = state[...] + scatter(total, ranks[0:1])
    copy = pltpu.make_async_copy(held, advanced, sem)
    copy.start()
    copy.wait()


def call(kernel, outs, args, flops, aliases={}):
    outs = [jax.ShapeDtypeStruct(shape, dtype) for shape, dtype in outs]
    return pl.pallas_call(
        kernel,
        out_shape=outs,
        input_output_aliases=aliases,
        compiler_params=pltpu.CompilerParams(vmem_limit_bytes=VMEM),
        cost_estimate=pl.CostEstimate(flops=flops, bytes_accessed=2**20, transcendentals=0),
    )(*args)


def swapped(block, axis, first):
    pairs = [(i, i + 1) for i in range(first, lax.axis_size(axis) - 1, 2)]
    return lax.ppermute(block, axis, pairs + [(j, i) for i, j in pairs])


def exchange(outgoing):
    wide_1, wide_0, narrow_1, narrow_0 = outgoing
    wide_1, narrow_1, wide_0, narrow_0 = [
        swapped(block, axis, first)
        for block, (axis, first) in zip((wide_1, narrow_1, wide_0, narrow_0), PHASES)
    ]
    return wide_1, wide_0, narrow_1, narrow_0


def local(state, neighbours, elem_tent, boundary, active, tent_height, volume_op, lift_op, trace_op):
    comps, elems = state.shape
    layers = active.shape[0]
    halo = boundary.shape[0]
    wide_len = halo // 3
    narrow_len = wide_len // 2
    boundary = boundary.reshape(-1, LANES)
    elem_tent = elem_tent.reshape(-1, LANES)
    tent_height = tent_height.reshape(1, -1)

    blocks = [((ROWS, width), BF16) for width in (wide_len, wide_len, narrow_len, narrow_len)]
    live = ((comps, MAX_LIVE), F32)
    all_columns = ((comps, elems), F32)
    args = (
        state, boundary, trace_op.transpose(1, 0, 2), neighbours, elem_tent, active, tent_height, volume_op,
        lift_op.transpose(2, 0, 1),
    )
    held = [jax.ShapeDtypeStruct(arg.shape, arg.dtype) for arg in args]
    outs = pl.pallas_call(
        first_kernel,
        in_specs=[pl.BlockSpec(memory_space=pltpu.MemorySpace.HBM)] * len(args),
        out_shape=[jax.ShapeDtypeStruct(shape, dtype) for shape, dtype in blocks] + held,
        scratch_shapes=[pltpu.SemaphoreType.DMA((len(args),))],
        compiler_params=pltpu.CompilerParams(vmem_limit_bytes=VMEM),
    )(*[pltpu.with_memory_space_constraint(arg, pltpu.MemorySpace.HBM) for arg in args])
    outgoing = outs[:4]
    state, boundary, trace, neighbours, elem_tent, active, tent_height, volume_op, lift = outs[4:]
    received = exchange(outgoing)
    compact, ranks, sent, base, kept, lift, trace, powers = call(
        local_first_kernel,
        [
            ((layers, 16, MAX_LIVE), F32),
            ((2 * layers, elems), I32),
            ((layers, halo), I32),
            live,
            live,
            ((comps, 4 * ROWS), BF16),
            ((4 * ROWS, comps), BF16),
            ((5 * POWER_ROWS, comps), BF16),
        ],
        (state, neighbours, elem_tent, boundary, active, tent_height, volume_op, lift, trace),
        10**6,
    )
    tables = [(compact.shape, F32), (ranks.shape, I32), (sent.shape, I32)]

    def layer(_, carry):
        received, outgoing, state, compact, ranks, sent, base, kept = carry
        delta, *outgoing = call(
            advance_kernel,
            [live] + blocks,
            (*received, *outgoing, compact, base, kept, sent, powers, lift, trace),
            10**6,
            {4 + i: 1 + i for i in range(4)},
        )
        received = exchange(outgoing)
        state, compact, ranks, sent, base, kept = call(
            local_kernel,
            [all_columns, *tables, live, live],
            (state, delta, compact, ranks, sent, volume_op, lift, trace),
            10**6,
            {0: 0, 2: 1, 3: 2, 4: 3},
        )
        return received, tuple(outgoing), state, compact, ranks, sent, base, kept

    received, _, state, compact, ranks, _, base, _ = lax.fori_loop(
        0, layers - 1, layer, (received, tuple(outgoing), state, compact, ranks, sent, base, kept)
    )
    return pl.pallas_call(
        last_kernel,
        out_specs=pl.BlockSpec(memory_space=pltpu.MemorySpace.HBM),
        out_shape=jax.ShapeDtypeStruct((comps, elems), F32),
        scratch_shapes=[pltpu.VMEM((comps, elems), F32), pltpu.SemaphoreType.DMA],
        compiler_params=pltpu.CompilerParams(vmem_limit_bytes=VMEM),
    )(*received, compact, base, ranks, powers, lift, state)


def solution(mesh):
    both = ("wide", "narrow")
    return jax.shard_map(
        local,
        mesh=mesh,
        in_specs=(P(None, both), P(None, both), P(both), P(both), P(None, both), P(both), P(), P(), P()),
        out_specs=P(None, both),
        check_vma=False,
    )
```

```python
import jax
import jax.numpy as jnp
from jax import lax
from jax.experimental import pallas as pl
from jax.experimental.pallas import tpu as pltpu
from jax.sharding import PartitionSpec as P

TENT_SIZE = 16
MAX_TENTS = 24
MAX_LIVE = TENT_SIZE * MAX_TENTS
ROWS = 64
BLOCK = 256
SPLIT = 256
CHUNK = 512
LANES = 128
VMEM = 24 * 2**20
POWER_ROWS = 112
PHASES = (("wide", 1), ("narrow", 1), ("wide", 0), ("narrow", 0))
BF16, F32, I32 = jnp.bfloat16, jnp.float32, jnp.int32


def mm(left, right):
    return jnp.dot(left, right, preferred_element_type=F32)


def mm_t(left, right):
    return lax.dot_general(left, right, (((1,), (1,)), ((), ())), preferred_element_type=F32)


def low_of(index):
    return index & (BLOCK - 1)


def high_of(index):
    return index >> 8


def hot(index, depth):
    low, high = low_of(index), high_of(index)
    rows = lax.broadcasted_iota(I32, (BLOCK, index.shape[1]), 0).astype(F32).astype(BF16)
    parts = []
    for b in range(-(-depth // BLOCK)):
        here = jnp.where(high == b, low, -1).astype(F32).astype(BF16)
        count = min(BLOCK, depth - b * BLOCK)
        parts.append(jnp.where(rows[:count] == here, jnp.ones((), BF16), jnp.zeros((), BF16)))
    return parts[0] if len(parts) == 1 else jnp.concatenate(parts, axis=0)


def choose(found, key, first, rows, default=None):
    count = found.shape[0] // rows
    total = found[(count - 1) * rows :]
    if default is not None:
        total = jnp.where(key == first + count - 1, total, default)
    for b in range(count - 2, -1, -1):
        total = jnp.where(key == first + b, found[b * rows : (b + 1) * rows], total)
    return total


def stack(table):
    return jnp.concatenate([table[:, at : at + BLOCK] for at in range(0, table.shape[1], BLOCK)], axis=0)


def pick(table, low, high, first=0, default=0.0):
    return choose(mm(stack(table), hot(low, BLOCK)), high, first, table.shape[0], default)


def two_parts(values):
    rows = values.shape[0]
    start = -(-rows // 16) * 16
    top = values.astype(BF16).astype(F32)
    gap = jnp.zeros((start - rows, values.shape[1]), F32)
    return jnp.concatenate([jnp.concatenate([top, gap], axis=0), values - top], axis=0).astype(BF16), start


def three_parts(values):
    top = values.astype(BF16).astype(F32)
    mid = (values - top).astype(BF16).astype(F32)
    return top, mid, values - top - mid


def even(axis):
    return lax.axis_index(axis) % 2 == 0


def by_phase(columns):
    half, quarter = columns.shape[1] // 3, columns.shape[1] // 6
    low, high = columns[:, :half], columns[:, half : 2 * half]
    left, right = columns[:, 2 * half : 2 * half + quarter], columns[:, 2 * half + quarter :]
    wide, narrow = even("wide"), even("narrow")
    return jnp.concatenate(
        [
            jnp.where(wide, low, high),
            jnp.where(wide, high, low),
            jnp.where(narrow, left, right),
            jnp.where(narrow, right, left),
        ],
        axis=1,
    )


def remote_by_phase(near, local_columns, halo):
    half, quarter = halo // 3, halo // 6
    at = near - local_columns
    wide, narrow = even("wide"), even("narrow")
    in_wide = jnp.where(wide, at, jnp.where(at < half, at + half, at - half))
    in_narrow = jnp.where(narrow, at, jnp.where(at < 2 * half + quarter, at + quarter, at - quarter))
    return jnp.where(at < 0, near, local_columns + jnp.where(at < 2 * half, in_wide, in_narrow))


def store_blocks(out, refs):
    at = 0
    for ref in refs:
        width = ref.shape[1]
        ref[...] = out[:, at : at + width].astype(BF16)
        at += width


def row_of(ref):
    return jnp.concatenate([ref[i : i + 1, :] for i in range(ref.shape[0])], axis=1)


def face_rows(op, face):
    gap = jnp.zeros((ROWS - op.shape[0], op.shape[2]), F32)
    return jnp.concatenate([op[:, face, :].astype(F32), gap], axis=0)


def first_kernel(*refs):
    count = (len(refs) - 4) // 2
    inputs, blocks, held, sems = refs[:count], refs[count : count + 4], refs[count + 4 : -1], refs[-1]
    copies = [pltpu.make_async_copy(src, dst, sems.at[i]) for i, (src, dst) in enumerate(zip(inputs, held))]
    for copy in copies:
        copy.start()
    state, boundary, trace_op = held[:3]
    copies[1].wait()
    at = by_phase(row_of(boundary))
    chosen, high = hot(low_of(at), BLOCK), high_of(at)
    copies[2].wait()
    face = face_rows(trace_op, 3).astype(BF16)
    copies[0].wait()
    traces = mm(face, state[...].astype(BF16)).astype(BF16)
    store_blocks(choose(mm(stack(traces), chosen), high, 0, ROWS), blocks)
    for copy in copies[3:]:
        copy.wait()


def make_index(neighbours, elem_tent, boundary, active, height, compact, ranks, sent):
    tent = row_of(elem_tent)
    elems = tent.shape[1]
    tents = height.shape[1]
    layers = active.shape[0]
    act = active[...].astype(F32)
    top, mid, low = three_parts(height[...])
    row = lax.broadcasted_iota(I32, (2 * layers, tents), 0)
    high_rows = jnp.where(row == 0, top, jnp.where(row == 1, mid, jnp.where(row == 2, low, 0.0)))
    found = mm(jnp.concatenate([act, act, high_rows], axis=0).astype(BF16), hot(tent, tents))
    live, high_rows = found[: 2 * layers], found[2 * layers :]
    upto = jnp.where(
        lax.broadcasted_iota(I32, (LANES, LANES), 0) <= lax.broadcasted_iota(I32, (LANES, LANES), 1), 1.0, 0.0
    ).astype(BF16)
    chunks = [live[:, at : at + LANES] for at in range(0, elems, LANES)]
    counts = mm(jnp.concatenate(chunks, axis=0).astype(BF16), upto)
    offset = jnp.zeros((2 * layers, 1), F32)
    parts = []
    for c in range(len(chunks)):
        part = counts[c * 2 * layers : (c + 1) * 2 * layers]
        parts.append(part + offset)
        offset = offset + part[:, LANES - 1 :]
    place = jnp.where(live > 0.5, jnp.concatenate(parts, axis=1), 0.0).astype(I32)
    ranks[...] = place - 1
    row = lax.broadcasted_iota(I32, (2 * layers, elems), 0)
    digits = jnp.where(row < layers, low_of(place), high_of(place)).astype(F32)
    table = jnp.concatenate([digits, jnp.zeros_like(digits)], axis=0).astype(BF16)
    at = by_phase(row_of(boundary))
    found = pick(table, low_of(at), high_of(at))
    sent[...] = (found[:layers] + BLOCK * found[layers : 2 * layers]).astype(I32) - 1

    near = remote_by_phase(neighbours[...], 4 * elems, at.shape[1])
    near = jnp.concatenate([near, near], axis=0)
    near = jnp.where(row < layers, low_of(near), high_of(near)).astype(F32)
    elem = lax.broadcasted_iota(I32, (2 * layers, elems), 1)
    own = jnp.where(row == 3, low_of(elem).astype(F32), jnp.where(row == 4, high_of(elem).astype(F32), 0.0))
    rows16 = jnp.concatenate([near, high_rows + own], axis=0)
    count = MAX_LIVE // LANES
    for l in range(0, layers, 2):
        tables, columns = [], []
        for m in (l, l + 1):
            rank = place[m : m + 1] - 1
            tables += [jnp.where(rank >> 7 == b, rows16, 0.0) for b in range(count)]
            columns.append(hot(jnp.where(rank < 0, -1, rank & (LANES - 1)), LANES))
        found = mm_t(jnp.concatenate(tables, axis=0).astype(BF16), jnp.concatenate(columns, axis=0))
        for m in (0, 1):
            for b in range(count):
                at = 16 * (m * count + b)
                compact[l + m, :, b * LANES : (b + 1) * LANES] = found[at : at + 16, m * LANES : (m + 1) * LANES]
            compact[l + m, 13:14, :LANES] = jnp.broadcast_to(offset[l + m : l + m + 1], (1, LANES))


def whole(compact, row, count, here):
    rows = [compact[i : i + 1, here] for i in range(row, row + count)]
    return (rows[0] if count == 1 else jnp.concatenate(rows, axis=1)).astype(I32)


def many(compact):
    return jnp.max(compact[13:14, :LANES]) > SPLIT


FIRST, OTHERS = slice(0, SPLIT), slice(SPLIT, MAX_LIVE)
ALL = slice(0, MAX_LIVE)


def by_face(columns):
    n = columns.shape[1] // 4
    return jnp.concatenate([columns[:, g * n : (g + 1) * n] for g in range(4)], axis=0)


def local_part(values, compact, here, volume, lift, trace, base, kept):
    comps, elems = values.shape
    blocks = elems // BLOCK
    count = here.stop - here.start
    parts, rows = two_parts(values)
    top = stack(parts[:rows])
    low = jnp.concatenate([whole(compact, 11, 1, here), whole(compact, 0, 4, here)], axis=1)
    high = jnp.concatenate([whole(compact, 12, 1, here), whole(compact, 4, 4, here)], axis=1)
    block, face = high & (blocks - 1), high // blocks
    near = []
    for at in range(0, low.shape[1], CHUNK):
        now = slice(at, at + CHUNK)
        near.append(choose(mm(top, hot(low[:, now], BLOCK)), block[:, now], 0, rows)[:comps].astype(BF16))
    near = jnp.concatenate(near, axis=1)
    mine, near, face = near[:, :count], near[:, count:], face[:, count:]
    picked = []
    for at in range(0, near.shape[1], CHUNK):
        now = slice(at, at + CHUNK)
        picked.append(choose(mm(trace[...], near[:, now]), face[:, now], 0, ROWS, 0.0))
    picked = by_face(jnp.concatenate(picked, axis=1)).astype(BF16)
    if kept is not None:
        rest = stack(jnp.concatenate([parts[rows:].astype(F32), jnp.zeros((rows - comps, elems), F32)], axis=0))
        rest = choose(mm(rest.astype(BF16), hot(low[:, :count], BLOCK)), block[:, :count], 0, rows)
        kept[:, here] = mine.astype(F32) + rest[:comps]
    base[:, here] = mm(volume[...], mine) + mm(lift[...], picked)


def local_parts(values, state, compact, *refs):
    local_part(values, compact, FIRST, *refs)
    for ref in refs[3:]:
        ref[:, OTHERS] = jnp.zeros((ref.shape[0], MAX_LIVE - SPLIT), F32)

    @pl.when(many(compact))
    def _():
        local_part(state[...], compact, OTHERS, *refs)


def local_first_kernel(
    state, neighbours, elem_tent, boundary, active, height, volume, lift_op, trace_op,
    compact, ranks, sent, base, kept, lift, trace, powers,
):
    powers[...] = powers_of(volume[...])
    make_index(neighbours, elem_tent, boundary, active, height, compact, ranks, sent)
    lifts = jnp.concatenate([face_rows(lift_op, g) for g in range(4)], axis=0).astype(BF16)
    comps = lifts.shape[1]
    diagonal = lax.broadcasted_iota(I32, (comps, comps), 0) == lax.broadcasted_iota(I32, (comps, comps), 1)
    lift[...] = mm_t(jnp.where(diagonal, 1.0, 0.0).astype(BF16), lifts).astype(BF16)
    trace[...] = jnp.concatenate([face_rows(trace_op, g) for g in range(4)], axis=0).astype(BF16)
    local_parts(state[...], state, compact[0], volume, lift, trace, base, kept)


def scatter(delta, rank, here):
    parts, second = two_parts(delta)
    found = mm(parts, hot(rank - here.start, delta.shape[1]))
    return found[: delta.shape[0]] + found[second:]


def local_kernel(
    state, delta, compact, ranks, sent, volume, lift, trace, new_state, new_compact, new_ranks, new_sent, base, kept
):
    values = state[...] + scatter(delta[...], ranks[0:1], ALL)
    new_state[...] = values
    tables = [compact[l] for l in range(1, compact.shape[0])]
    for l, table in enumerate(tables):
        new_compact[l] = table
    later_ranks, later_sent = ranks[1:], sent[1:]
    new_ranks[:-1, :] = later_ranks
    new_sent[:-1, :] = later_sent
    local_parts(values, new_state, tables[0], volume, lift, trace, base, kept)


def powers_of(volume):
    gap = jnp.zeros((POWER_ROWS - volume.shape[0], volume.shape[1]), F32)
    parts = [volume.astype(F32)]
    for _ in range(2):
        power = sum(mm(part.astype(BF16), volume) for part in parts[-2:])
        top = power.astype(BF16).astype(F32)
        parts += [top, power - top]
    return jnp.concatenate([half for part in parts for half in (part, gap)], axis=0).astype(BF16)


def taylor_terms(received, compact, here, base, powers, lift):
    remote = jnp.concatenate([ref[...] for ref in received], axis=1)
    first_block = 4 * 1024 // BLOCK
    picked = by_face(pick(remote, whole(compact, 0, 4, here), whole(compact, 4, 4, here), first_block)).astype(BF16)
    heights = compact[8:9, here] + compact[9:10, here] + compact[10:11, here]
    first = heights * (base[:, here] + mm(lift[...], picked))
    found = mm(powers[...], first.astype(BF16))
    comps = first.shape[0]
    products = [found[at : at + comps] for at in range(0, found.shape[0], POWER_ROWS)]
    total, scale = first, 1.0
    for order, product in ((2, products[0]), (3, products[1] + products[2]), (4, products[3] + products[4])):
        scale = scale * (heights / order)
        total = total + scale * product
    return total


def advance_kernel(r0, r1, r2, r3, o0, o1, o2, o3, compact, base, kept, sent, powers, lift, trace, delta, *outgoing):
    place = sent[0:1]
    chosen, high = hot(low_of(place), BLOCK), high_of(place)
    total = taylor_terms((r0, r1, r2, r3), compact[0], ALL, base, powers, lift)
    delta[...] = total
    traces = mm(trace[3 * ROWS :, :], (kept[...] + total).astype(BF16))
    rest = -MAX_LIVE % BLOCK
    table = jnp.concatenate([traces, jnp.zeros((ROWS, rest), F32)], axis=1).astype(BF16)
    before = jnp.concatenate([o0[...], o1[...], o2[...], o3[...]], axis=1).astype(F32)
    store_blocks(choose(mm(stack(table), chosen), high, 0, ROWS, before), outgoing)


def last_kernel(r0, r1, r2, r3, compact, base, ranks, powers, lift, state, advanced, held, sem):
    rows = compact[0]

    def part(here, before):
        total = taylor_terms((r0, r1, r2, r3), rows, here, base, powers, lift)
        held[...] = before[...] + scatter(total, ranks[0:1], here)

    part(FIRST, state)

    @pl.when(many(rows))
    def _():
        part(OTHERS, held)

    copy = pltpu.make_async_copy(held, advanced, sem)
    copy.start()
    copy.wait()


def call(kernel, outs, args, flops, aliases={}):
    outs = [jax.ShapeDtypeStruct(shape, dtype) for shape, dtype in outs]
    return pl.pallas_call(
        kernel,
        out_shape=outs,
        input_output_aliases=aliases,
        compiler_params=pltpu.CompilerParams(vmem_limit_bytes=VMEM),
        cost_estimate=pl.CostEstimate(flops=flops, bytes_accessed=2**20, transcendentals=0),
    )(*args)


def swapped(block, axis, first):
    pairs = [(i, i + 1) for i in range(first, lax.axis_size(axis) - 1, 2)]
    return lax.ppermute(block, axis, pairs + [(j, i) for i, j in pairs])


def exchange(outgoing):
    wide_1, wide_0, narrow_1, narrow_0 = outgoing
    wide_1, narrow_1, wide_0, narrow_0 = [
        swapped(block, axis, first)
        for block, (axis, first) in zip((wide_1, narrow_1, wide_0, narrow_0), PHASES)
    ]
    return wide_1, wide_0, narrow_1, narrow_0


def local(state, neighbours, elem_tent, boundary, active, tent_height, volume_op, lift_op, trace_op):
    comps, elems = state.shape
    layers = active.shape[0]
    halo = boundary.shape[0]
    wide_len = halo // 3
    narrow_len = wide_len // 2
    boundary = boundary.reshape(-1, LANES)
    elem_tent = elem_tent.reshape(-1, LANES)
    tent_height = tent_height.reshape(1, -1)

    blocks = [((ROWS, width), BF16) for width in (wide_len, wide_len, narrow_len, narrow_len)]
    live = ((comps, MAX_LIVE), F32)
    all_columns = ((comps, elems), F32)
    args = (
        state, boundary, trace_op.transpose(1, 0, 2), neighbours, elem_tent, active, tent_height, volume_op,
        lift_op.transpose(2, 0, 1),
    )
    held = [jax.ShapeDtypeStruct(arg.shape, arg.dtype) for arg in args]
    outs = pl.pallas_call(
        first_kernel,
        in_specs=[pl.BlockSpec(memory_space=pltpu.MemorySpace.HBM)] * len(args),
        out_shape=[jax.ShapeDtypeStruct(shape, dtype) for shape, dtype in blocks] + held,
        scratch_shapes=[pltpu.SemaphoreType.DMA((len(args),))],
        compiler_params=pltpu.CompilerParams(vmem_limit_bytes=VMEM),
    )(*[pltpu.with_memory_space_constraint(arg, pltpu.MemorySpace.HBM) for arg in args])
    outgoing = outs[:4]
    state, boundary, trace, neighbours, elem_tent, active, tent_height, volume_op, lift = outs[4:]
    received = exchange(outgoing)
    compact, ranks, sent, base, kept, lift, trace, powers = call(
        local_first_kernel,
        [
            ((layers, 16, MAX_LIVE), F32),
            ((2 * layers, elems), I32),
            ((layers, halo), I32),
            live,
            live,
            ((comps, 4 * ROWS), BF16),
            ((4 * ROWS, comps), BF16),
            ((5 * POWER_ROWS, comps), BF16),
        ],
        (state, neighbours, elem_tent, boundary, active, tent_height, volume_op, lift, trace),
        10**6,
    )
    tables = [(compact.shape, F32), (ranks.shape, I32), (sent.shape, I32)]

    def layer(_, carry):
        received, outgoing, state, compact, ranks, sent, base, kept = carry
        delta, *outgoing = call(
            advance_kernel,
            [live] + blocks,
            (*received, *outgoing, compact, base, kept, sent, powers, lift, trace),
            10**6,
            {4 + i: 1 + i for i in range(4)},
        )
        received = exchange(outgoing)
        state, compact, ranks, sent, base, kept = call(
            local_kernel,
            [all_columns, *tables, live, live],
            (state, delta, compact, ranks, sent, volume_op, lift, trace),
            10**6,
            {0: 0, 2: 1, 3: 2, 4: 3},
        )
        return received, tuple(outgoing), state, compact, ranks, sent, base, kept

    received, _, state, compact, ranks, _, base, _ = lax.fori_loop(
        0, layers - 1, layer, (received, tuple(outgoing), state, compact, ranks, sent, base, kept)
    )
    return pl.pallas_call(
        last_kernel,
        out_specs=pl.BlockSpec(memory_space=pltpu.MemorySpace.HBM),
        out_shape=jax.ShapeDtypeStruct((comps, elems), F32),
        scratch_shapes=[pltpu.VMEM((comps, elems), F32), pltpu.SemaphoreType.DMA],
        compiler_params=pltpu.CompilerParams(vmem_limit_bytes=VMEM),
    )(*received, compact, base, ranks, powers, lift, state)


def solution(mesh):
    both = ("wide", "narrow")
    return jax.shard_map(
        local,
        mesh=mesh,
        in_specs=(P(None, both), P(None, both), P(both), P(both), P(None, both), P(both), P(), P(), P()),
        out_specs=P(None, both),
        check_vma=False,
    )
```

```python
import jax
import jax.numpy as jnp
from jax import lax
from jax.experimental import pallas as pl
from jax.experimental.pallas import tpu as pltpu
from jax.sharding import PartitionSpec as P

TENT_SIZE = 16
MAX_TENTS = 24
MAX_LIVE = TENT_SIZE * MAX_TENTS
ROWS = 64
BLOCK = 256
SPLIT = 256
CHUNK = 512
LANES = 128
VMEM = 24 * 2**20
POWER_ROWS = 112
PHASES = (("wide", 1), ("narrow", 1), ("wide", 0), ("narrow", 0))
BF16, F32, I32 = jnp.bfloat16, jnp.float32, jnp.int32


def mm(left, right):
    return jnp.dot(left, right, preferred_element_type=F32)


def mm_t(left, right):
    return lax.dot_general(left, right, (((1,), (1,)), ((), ())), preferred_element_type=F32)


def low_of(index):
    return index & (BLOCK - 1)


def high_of(index):
    return index >> 8


def hot(index, depth):
    low, high = low_of(index), high_of(index)
    rows = lax.broadcasted_iota(I32, (BLOCK, index.shape[1]), 0).astype(F32).astype(BF16)
    parts = []
    for b in range(-(-depth // BLOCK)):
        here = jnp.where(high == b, low, -1).astype(F32).astype(BF16)
        count = min(BLOCK, depth - b * BLOCK)
        parts.append(jnp.where(rows[:count] == here, jnp.ones((), BF16), jnp.zeros((), BF16)))
    return parts[0] if len(parts) == 1 else jnp.concatenate(parts, axis=0)


def choose(found, key, first, rows, default=None):
    count = found.shape[0] // rows
    total = found[(count - 1) * rows :]
    if default is not None:
        total = jnp.where(key == first + count - 1, total, default)
    for b in range(count - 2, -1, -1):
        total = jnp.where(key == first + b, found[b * rows : (b + 1) * rows], total)
    return total


def stack(table):
    return jnp.concatenate([table[:, at : at + BLOCK] for at in range(0, table.shape[1], BLOCK)], axis=0)


def pick(table, low, high, first=0, default=0.0):
    return choose(mm(stack(table), hot(low, BLOCK)), high, first, table.shape[0], default)


def two_parts(values):
    rows = values.shape[0]
    start = -(-rows // 16) * 16
    top = values.astype(BF16).astype(F32)
    gap = jnp.zeros((start - rows, values.shape[1]), F32)
    return jnp.concatenate([top, gap, values - top, gap], axis=0).astype(BF16), start


def three_parts(values):
    top = values.astype(BF16).astype(F32)
    mid = (values - top).astype(BF16).astype(F32)
    return top, mid, values - top - mid


def even(axis):
    return lax.axis_index(axis) % 2 == 0


def by_phase(columns):
    half, quarter = columns.shape[1] // 3, columns.shape[1] // 6
    low, high = columns[:, :half], columns[:, half : 2 * half]
    left, right = columns[:, 2 * half : 2 * half + quarter], columns[:, 2 * half + quarter :]
    wide, narrow = even("wide"), even("narrow")
    return jnp.concatenate(
        [
            jnp.where(wide, low, high),
            jnp.where(wide, high, low),
            jnp.where(narrow, left, right),
            jnp.where(narrow, right, left),
        ],
        axis=1,
    )


def remote_by_phase(near, local_columns, halo):
    half, quarter = halo // 3, halo // 6
    at = near - local_columns
    wide, narrow = even("wide"), even("narrow")
    in_wide = jnp.where(wide, at, jnp.where(at < half, at + half, at - half))
    in_narrow = jnp.where(narrow, at, jnp.where(at < 2 * half + quarter, at + quarter, at - quarter))
    return jnp.where(at < 0, near, local_columns + jnp.where(at < 2 * half, in_wide, in_narrow))


def store_blocks(out, refs):
    at = 0
    for ref in refs:
        width = ref.shape[1]
        ref[...] = out[:, at : at + width].astype(BF16)
        at += width


def row_of(ref):
    return jnp.concatenate([ref[i : i + 1, :] for i in range(ref.shape[0])], axis=1)


def face_rows(op, face):
    gap = jnp.zeros((ROWS - op.shape[0], op.shape[2]), F32)
    return jnp.concatenate([op[:, face, :].astype(F32), gap], axis=0)


def first_kernel(*refs):
    count = (len(refs) - 4) // 2
    inputs, blocks, held, sems = refs[:count], refs[count : count + 4], refs[count + 4 : -1], refs[-1]
    copies = [pltpu.make_async_copy(src, dst, sems.at[i]) for i, (src, dst) in enumerate(zip(inputs, held))]
    for copy in copies:
        copy.start()
    state, boundary, trace_op = held[:3]
    copies[1].wait()
    at = by_phase(row_of(boundary))
    chosen, high = hot(low_of(at), BLOCK), high_of(at)
    copies[2].wait()
    face = face_rows(trace_op, 3).astype(BF16)
    copies[0].wait()
    traces = mm(face, state[...].astype(BF16)).astype(BF16)
    store_blocks(choose(mm(stack(traces), chosen), high, 0, ROWS), blocks)
    for copy in copies[3:]:
        copy.wait()


def make_index(neighbours, elem_tent, boundary, active, height, compact, ranks, sent):
    tent = row_of(elem_tent)
    elems = tent.shape[1]
    tents = height.shape[1]
    layers = active.shape[0]
    act = active[...].astype(F32)
    top, mid, low = three_parts(height[...])
    row = lax.broadcasted_iota(I32, (2 * layers, tents), 0)
    high_rows = jnp.where(row == 0, top, jnp.where(row == 1, mid, jnp.where(row == 2, low, 0.0)))
    found = mm(jnp.concatenate([act, act, high_rows], axis=0).astype(BF16), hot(tent, tents))
    live, high_rows = found[: 2 * layers], found[2 * layers :]
    upto = jnp.where(
        lax.broadcasted_iota(I32, (LANES, LANES), 0) <= lax.broadcasted_iota(I32, (LANES, LANES), 1), 1.0, 0.0
    ).astype(BF16)
    chunks = [live[:, at : at + LANES] for at in range(0, elems, LANES)]
    counts = mm(jnp.concatenate(chunks, axis=0).astype(BF16), upto)
    offset = jnp.zeros((2 * layers, 1), F32)
    parts = []
    for c in range(len(chunks)):
        part = counts[c * 2 * layers : (c + 1) * 2 * layers]
        parts.append(part + offset)
        offset = offset + part[:, LANES - 1 :]
    place = jnp.where(live > 0.5, jnp.concatenate(parts, axis=1), 0.0).astype(I32)
    ranks[...] = place - 1
    row = lax.broadcasted_iota(I32, (2 * layers, elems), 0)
    digits = jnp.where(row < layers, low_of(place), high_of(place)).astype(F32)
    table = jnp.concatenate([digits, jnp.zeros_like(digits)], axis=0).astype(BF16)
    at = by_phase(row_of(boundary))
    found = pick(table, low_of(at), high_of(at))
    sent[...] = (found[:layers] + BLOCK * found[layers : 2 * layers]).astype(I32) - 1

    near = remote_by_phase(neighbours[...], 4 * elems, at.shape[1])
    near = jnp.concatenate([near, near], axis=0)
    near = jnp.where(row < layers, low_of(near), high_of(near)).astype(F32)
    elem = lax.broadcasted_iota(I32, (2 * layers, elems), 1)
    own = jnp.where(row == 3, low_of(elem).astype(F32), jnp.where(row == 4, high_of(elem).astype(F32), 0.0))
    rows16 = jnp.concatenate([near, high_rows + own], axis=0)
    count = MAX_LIVE // LANES
    for l in range(0, layers, 2):
        tables, columns = [], []
        for m in (l, l + 1):
            rank = place[m : m + 1] - 1
            tables += [jnp.where(rank >> 7 == b, rows16, 0.0) for b in range(count)]
            columns.append(hot(jnp.where(rank < 0, -1, rank & (LANES - 1)), LANES))
        found = mm_t(jnp.concatenate(tables, axis=0).astype(BF16), jnp.concatenate(columns, axis=0))
        for m in (0, 1):
            for b in range(count):
                at = 16 * (m * count + b)
                compact[l + m, :, b * LANES : (b + 1) * LANES] = found[at : at + 16, m * LANES : (m + 1) * LANES]
            compact[l + m, 13:14, :LANES] = jnp.broadcast_to(offset[l + m : l + m + 1], (1, LANES))


def whole(compact, row, count, here):
    rows = [compact[i : i + 1, here] for i in range(row, row + count)]
    return (rows[0] if count == 1 else jnp.concatenate(rows, axis=1)).astype(I32)


def many(compact):
    return jnp.max(compact[13:14, :LANES]) > SPLIT


FIRST, OTHERS = slice(0, SPLIT), slice(SPLIT, MAX_LIVE)
ALL = slice(0, MAX_LIVE)


def by_face(columns):
    n = columns.shape[1] // 4
    return jnp.concatenate([columns[:, g * n : (g + 1) * n] for g in range(4)], axis=0)


def local_part(values, compact, here, volume, lift, trace, base, kept):
    comps, elems = values.shape
    blocks = elems // BLOCK
    count = here.stop - here.start
    parts, rows = two_parts(values)
    top = stack(parts[:rows])
    low = jnp.concatenate([whole(compact, 11, 1, here), whole(compact, 0, 4, here)], axis=1)
    high = jnp.concatenate([whole(compact, 12, 1, here), whole(compact, 4, 4, here)], axis=1)
    block, face = high & (blocks - 1), high // blocks
    near = []
    for at in range(0, low.shape[1], CHUNK):
        now = slice(at, at + CHUNK)
        near.append(choose(mm(top, hot(low[:, now], BLOCK)), block[:, now], 0, rows)[:comps].astype(BF16))
    near = jnp.concatenate(near, axis=1)
    mine, near, face = near[:, :count], near[:, count:], face[:, count:]
    picked = []
    for at in range(0, near.shape[1], CHUNK):
        now = slice(at, at + CHUNK)
        picked.append(choose(mm(trace[...], near[:, now]), face[:, now], 0, ROWS, 0.0))
    picked = by_face(jnp.concatenate(picked, axis=1)).astype(BF16)
    if kept is not None:
        rest = choose(mm(stack(parts[rows:]), hot(low[:, :count], BLOCK)), block[:, :count], 0, rows)
        kept[:, here] = mine.astype(F32) + rest[:comps]
    base[:, here] = mm(volume[...], mine) + mm(lift[...], picked)


def local_parts(values, state, compact, *refs):
    local_part(values, compact, FIRST, *refs)
    for ref in refs[3:]:
        ref[:, OTHERS] = jnp.zeros((ref.shape[0], MAX_LIVE - SPLIT), F32)

    @pl.when(many(compact))
    def _():
        local_part(state[...], compact, OTHERS, *refs)


def local_first_kernel(
    state, neighbours, elem_tent, boundary, active, height, volume, lift_op, trace_op,
    compact, ranks, sent, base, kept, lift, trace, powers,
):
    powers[...] = powers_of(volume[...])
    make_index(neighbours, elem_tent, boundary, active, height, compact, ranks, sent)
    lifts = jnp.concatenate([face_rows(lift_op, g) for g in range(4)], axis=0).astype(BF16)
    comps = lifts.shape[1]
    diagonal = lax.broadcasted_iota(I32, (comps, comps), 0) == lax.broadcasted_iota(I32, (comps, comps), 1)
    lift[...] = mm_t(jnp.where(diagonal, 1.0, 0.0).astype(BF16), lifts).astype(BF16)
    trace[...] = jnp.concatenate([face_rows(trace_op, g) for g in range(4)], axis=0).astype(BF16)
    local_parts(state[...], state, compact[0], volume, lift, trace, base, kept)


def scatter(delta, rank, here):
    parts, second = two_parts(delta)
    found = mm(parts, hot(rank - here.start, delta.shape[1]))
    return found[: delta.shape[0]] + found[second : second + delta.shape[0]]


def local_kernel(
    state, delta, compact, ranks, sent, volume, lift, trace, new_state, new_compact, new_ranks, new_sent, base, kept
):
    values = state[...] + scatter(delta[...], ranks[0:1], ALL)
    new_state[...] = values
    tables = [compact[l] for l in range(1, compact.shape[0])]
    for l, table in enumerate(tables):
        new_compact[l] = table
    later_ranks, later_sent = ranks[1:], sent[1:]
    new_ranks[:-1, :] = later_ranks
    new_sent[:-1, :] = later_sent
    local_parts(values, new_state, tables[0], volume, lift, trace, base, kept)


def powers_of(volume):
    gap = jnp.zeros((POWER_ROWS - volume.shape[0], volume.shape[1]), F32)
    parts = [volume.astype(F32)]
    for _ in range(2):
        power = sum(mm(part.astype(BF16), volume) for part in parts[-2:])
        top = power.astype(BF16).astype(F32)
        parts += [top, power - top]
    return jnp.concatenate([half for part in parts for half in (part, gap)], axis=0).astype(BF16)


def taylor_terms(received, compact, here, base, powers, lift):
    remote = jnp.concatenate([ref[...] for ref in received], axis=1)
    first_block = 4 * 1024 // BLOCK
    picked = by_face(pick(remote, whole(compact, 0, 4, here), whole(compact, 4, 4, here), first_block)).astype(BF16)
    heights = compact[8:9, here] + compact[9:10, here] + compact[10:11, here]
    first = heights * (base[:, here] + mm(lift[...], picked))
    found = mm(powers[...], first.astype(BF16))
    comps = first.shape[0]
    products = [found[at : at + comps] for at in range(0, found.shape[0], POWER_ROWS)]
    total, scale = first, 1.0
    for order, product in ((2, products[0]), (3, products[1] + products[2]), (4, products[3] + products[4])):
        scale = scale * (heights / order)
        total = total + scale * product
    return total


def advance_kernel(r0, r1, r2, r3, o0, o1, o2, o3, compact, base, kept, sent, powers, lift, trace, delta, *outgoing):
    place = sent[0:1]
    chosen, high = hot(low_of(place), BLOCK), high_of(place)
    total = taylor_terms((r0, r1, r2, r3), compact[0], ALL, base, powers, lift)
    delta[...] = total
    traces = mm(trace[3 * ROWS :, :], (kept[...] + total).astype(BF16))
    rest = -MAX_LIVE % BLOCK
    table = jnp.concatenate([traces, jnp.zeros((ROWS, rest), F32)], axis=1).astype(BF16)
    before = jnp.concatenate([o0[...], o1[...], o2[...], o3[...]], axis=1).astype(F32)
    store_blocks(choose(mm(stack(table), chosen), high, 0, ROWS, before), outgoing)


def last_kernel(r0, r1, r2, r3, compact, base, ranks, powers, lift, state, advanced, held, sem):
    rows = compact[0]

    def part(here, before):
        total = taylor_terms((r0, r1, r2, r3), rows, here, base, powers, lift)
        held[...] = before[...] + scatter(total, ranks[0:1], here)

    part(FIRST, state)

    @pl.when(many(rows))
    def _():
        part(OTHERS, held)

    copy = pltpu.make_async_copy(held, advanced, sem)
    copy.start()
    copy.wait()


def call(kernel, outs, args, flops, aliases={}):
    outs = [jax.ShapeDtypeStruct(shape, dtype) for shape, dtype in outs]
    return pl.pallas_call(
        kernel,
        out_shape=outs,
        input_output_aliases=aliases,
        compiler_params=pltpu.CompilerParams(vmem_limit_bytes=VMEM),
        cost_estimate=pl.CostEstimate(flops=flops, bytes_accessed=2**20, transcendentals=0),
    )(*args)


def swapped(block, axis, first):
    pairs = [(i, i + 1) for i in range(first, lax.axis_size(axis) - 1, 2)]
    return lax.ppermute(block, axis, pairs + [(j, i) for i, j in pairs])


def exchange(outgoing):
    wide_1, wide_0, narrow_1, narrow_0 = outgoing
    wide_1, narrow_1, wide_0, narrow_0 = [
        swapped(block, axis, first)
        for block, (axis, first) in zip((wide_1, narrow_1, wide_0, narrow_0), PHASES)
    ]
    return wide_1, wide_0, narrow_1, narrow_0


def local(state, neighbours, elem_tent, boundary, active, tent_height, volume_op, lift_op, trace_op):
    comps, elems = state.shape
    layers = active.shape[0]
    halo = boundary.shape[0]
    wide_len = halo // 3
    narrow_len = wide_len // 2
    boundary = boundary.reshape(-1, LANES)
    elem_tent = elem_tent.reshape(-1, LANES)
    tent_height = tent_height.reshape(1, -1)

    blocks = [((ROWS, width), BF16) for width in (wide_len, wide_len, narrow_len, narrow_len)]
    live = ((comps, MAX_LIVE), F32)
    all_columns = ((comps, elems), F32)
    args = (
        state, boundary, trace_op.transpose(1, 0, 2), neighbours, elem_tent, active, tent_height, volume_op,
        lift_op.transpose(2, 0, 1),
    )
    held = [jax.ShapeDtypeStruct(arg.shape, arg.dtype) for arg in args]
    outs = pl.pallas_call(
        first_kernel,
        in_specs=[pl.BlockSpec(memory_space=pltpu.MemorySpace.HBM)] * len(args),
        out_shape=[jax.ShapeDtypeStruct(shape, dtype) for shape, dtype in blocks] + held,
        scratch_shapes=[pltpu.SemaphoreType.DMA((len(args),))],
        compiler_params=pltpu.CompilerParams(vmem_limit_bytes=VMEM),
    )(*[pltpu.with_memory_space_constraint(arg, pltpu.MemorySpace.HBM) for arg in args])
    outgoing = outs[:4]
    state, boundary, trace, neighbours, elem_tent, active, tent_height, volume_op, lift = outs[4:]
    received = exchange(outgoing)
    compact, ranks, sent, base, kept, lift, trace, powers = call(
        local_first_kernel,
        [
            ((layers, 16, MAX_LIVE), F32),
            ((2 * layers, elems), I32),
            ((layers, halo), I32),
            live,
            live,
            ((comps, 4 * ROWS), BF16),
            ((4 * ROWS, comps), BF16),
            ((5 * POWER_ROWS, comps), BF16),
        ],
        (state, neighbours, elem_tent, boundary, active, tent_height, volume_op, lift, trace),
        10**6,
    )
    tables = [(compact.shape, F32), (ranks.shape, I32), (sent.shape, I32)]

    def layer(_, carry):
        received, outgoing, state, compact, ranks, sent, base, kept = carry
        delta, *outgoing = call(
            advance_kernel,
            [live] + blocks,
            (*received, *outgoing, compact, base, kept, sent, powers, lift, trace),
            10**6,
            {4 + i: 1 + i for i in range(4)},
        )
        received = exchange(outgoing)
        state, compact, ranks, sent, base, kept = call(
            local_kernel,
            [all_columns, *tables, live, live],
            (state, delta, compact, ranks, sent, volume_op, lift, trace),
            10**6,
            {0: 0, 2: 1, 3: 2, 4: 3},
        )
        return received, tuple(outgoing), state, compact, ranks, sent, base, kept

    received, _, state, compact, ranks, _, base, _ = lax.fori_loop(
        0, layers - 1, layer, (received, tuple(outgoing), state, compact, ranks, sent, base, kept)
    )
    return pl.pallas_call(
        last_kernel,
        out_specs=pl.BlockSpec(memory_space=pltpu.MemorySpace.HBM),
        out_shape=jax.ShapeDtypeStruct((comps, elems), F32),
        scratch_shapes=[pltpu.VMEM((comps, elems), F32), pltpu.SemaphoreType.DMA],
        compiler_params=pltpu.CompilerParams(vmem_limit_bytes=VMEM),
    )(*received, compact, base, ranks, powers, lift, state)


def solution(mesh):
    both = ("wide", "narrow")
    return jax.shard_map(
        local,
        mesh=mesh,
        in_specs=(P(None, both), P(None, both), P(both), P(both), P(None, both), P(both), P(), P(), P()),
        out_specs=P(None, both),
        check_vma=False,
    )
```
